1024 devices in a mesh: cells: 128 (over y, z_lo, core), inst: 8 (over x, z_hi).
Axes of the slice: x: 4, y: 8, z: 16 (z_hi: 2, z_lo: 8; z = z_hi * 8 + z_lo), core: 2. Of those that a mesh axis runs over, the one named last changes fastest.
Arguments:
- state: float32 [16, 5, 2048, 512], P('inst', None, 'cells'), may hold values from -1 to 6, as said below
- wall_distance: float32 [2048, 512], P('cells'), may hold values from 1 to 8
- blade_counts: int32 [2], replicated, may hold values from 30 to 90
Outputs:
- increment: float32 [16, 5, 2048, 512], P('inst', None, 'cells')
The draws below stay inside these ranges and needn't reach their ends.
Inputs may be any that keep to these rules, and one draw needn't show every extreme that they name: `state`: each cell holds density, x and y momentum, total energy and density times the turbulence variable of a gas with heat ratio 1.4; density lies in 0.8 to 1.25, pressure in 0.6 to 1.4.
All inputs are finite; a program needn't handle non-finite values.
Results may differ from the reference program's by a relative error of at most 0.0003.
Values sent between devices are 32-bit elements; how exact they have to be, the bound alone decides.
No kernel may reach another device: no remote copies, remote signals or barrier semaphores. Data moves between devices by JAX's collectives and lax.ppermute only.
A program may use at most 32 MiB of HBM per device.

```python
import math
import jax
import jax.numpy as jnp
from jax import lax

NT = 16
CI = 512
NJ = 2048


def draw_state(key, part):
    keys = jax.random.split(key, 5)
    shape = (NT, NJ, CI)
    density = jax.random.uniform(keys[0], shape, jnp.float32, 0.8, 1.25)
    pressure = jax.random.uniform(keys[1], shape, jnp.float32, 0.6, 1.4)
    velocity_x = 0.5 + 0.25 * jax.random.truncated_normal(keys[2], -3.0, 3.0, shape, jnp.float32)
    velocity_y = 0.2 + 0.25 * jax.random.truncated_normal(keys[3], -3.0, 3.0, shape, jnp.float32)
    viscosity = jnp.exp(jax.random.uniform(keys[4], shape, jnp.float32, math.log(0.3), math.log(3.0)))
    energy = pressure / 0.4 + 0.5 * density * (velocity_x * velocity_x + velocity_y * velocity_y)
    return jnp.stack([density, density * velocity_x, density * velocity_y, energy, density * viscosity], 1)


def block_levels(own_key, shape, cuts, smallest, largest):
    gain, own = 1.0, jax.random.fold_in(own_key, 6)
    for dim, shards_of in cuts:
        steps = jnp.exp(jax.random.uniform(jax.random.fold_in(own, dim), (shards_of,), jnp.float32, smallest / len(cuts), largest / len(cuts)))
        gain = gain * jnp.repeat(steps, shape[dim] // shards_of).reshape([-1 if axis == dim else 1 for axis in range(len(shape))])
    return gain


def setup_inputs(seed: int = 0) -> dict:
    streams_of = jax.random.split(jax.random.key(seed), 4)
    return {
        "state": draw_state(jax.random.fold_in(streams_of[3], 71), 0),
        "wall_distance": jnp.clip(jnp.exp(math.log(8.0) - 2.0794415 * jax.random.uniform(streams_of[1], (NJ, CI), jnp.float32) ** block_levels(streams_of[1], (NJ, CI), ((0, 128),), -0.2, 0.2)), 1.0, 8.0),
        "blade_counts": jax.random.randint(streams_of[2], (2,), 30, 91).astype(jnp.int32),
    }


GAMMA_GAS = 1.4
ROTATION = 0.001
DESTRUCTION = 0.4
SEGMENT_WEIGHTS = (0.25, 1.0 / 6.0, 0.375, 0.5, 1.0)

def derivative_matrix(count):
    half = count // 2
    angles = 2.0 * math.pi * jnp.arange(count, dtype=jnp.float32) / count
    spread = angles[:, None] - angles[None, :]
    orders = jnp.arange(1, half, dtype=jnp.float32)
    terms = orders[None, None, :] * jnp.sin(orders[None, None, :] * spread[:, :, None])
    return -(2.0 / count) * lax.optimization_barrier(jnp.sum(terms, axis=2))

def lag_matrix(count, shift):
    half = count // 2
    angles = 2.0 * math.pi * jnp.arange(count, dtype=jnp.float32) / count
    spread = angles[:, None] - angles[None, :] + shift
    orders = jnp.arange(1, half, dtype=jnp.float32)
    terms = jnp.cos(orders[None, None, :] * spread[:, :, None])
    return (1.0 + 2.0 * lax.optimization_barrier(jnp.sum(terms, axis=2)) + jnp.cos(half * spread)) / count

def speeds(field):
    density = field[:, 0]
    velocity_x = field[:, 1] / density
    velocity_y = field[:, 2] / density
    pressure = (GAMMA_GAS - 1.0) * (field[:, 3] - 0.5 * (field[:, 1] * velocity_x + field[:, 2] * velocity_y))
    sound = jnp.sqrt(GAMMA_GAS * pressure / density)
    return (jnp.abs(velocity_x) + sound, jnp.abs(velocity_y) + sound)

def fluxes(field):
    density = field[:, 0]
    flow_x = field[:, 1]
    flow_y = field[:, 2]
    energy = field[:, 3]
    turbulent = field[:, 4]
    velocity_x = flow_x / density
    velocity_y = flow_y / density
    pressure = (GAMMA_GAS - 1.0) * (energy - 0.5 * (flow_x * velocity_x + flow_y * velocity_y))
    enthalpy = energy + pressure
    along_x = jnp.stack([flow_x, flow_x * velocity_x + pressure, flow_y * velocity_x, enthalpy * velocity_x, turbulent * velocity_x], 1)
    along_y = jnp.stack([flow_y, flow_x * velocity_y, flow_y * velocity_y + pressure, enthalpy * velocity_y, turbulent * velocity_y], 1)
    return (along_x, along_y)

def residual(padded, wave_max, distance):
    widened = jnp.concatenate([padded[..., :1], padded, padded[..., -1:]], axis=-1)
    along_x, along_y = fluxes(widened)
    inner = widened[:, :, 1:-1]
    flux_x = along_x[:, :, 1:-1]
    face_x = 0.5 * (flux_x[..., :-1] + flux_x[..., 1:]) - 0.5 * wave_max * (inner[..., 1:] - inner[..., :-1])
    middle = widened[..., 1:-1]
    flux_y = along_y[..., 1:-1]
    face_y = 0.5 * (flux_y[:, :, :-1] + flux_y[:, :, 1:]) - 0.5 * wave_max * (middle[:, :, 1:] - middle[:, :, :-1])
    balance = face_x[..., 1:] - face_x[..., :-1] + (face_y[:, :, 1:] - face_y[:, :, :-1])
    cells_now = padded[:, :, 1:-1]
    decay = DESTRUCTION * cells_now[:, 4] * cells_now[:, 4] / (cells_now[:, 0] * distance * distance)
    return jnp.concatenate([balance[:, :4], balance[:, 4:] + decay[:, None]], 1)

def reference(state, wall_distance, blade_counts):
    counts = blade_counts.astype(jnp.float32)
    omega = 2.0 * math.pi * ROTATION * counts[1]
    sigma = 2.0 * math.pi * counts[1] / counts[0]
    derivative = derivative_matrix(NT) * omega
    source = jnp.einsum('nm,mvji->nvji', derivative, state, precision=lax.Precision.HIGHEST)
    speed_x, speed_y = speeds(state)
    wave_max = jnp.max(jnp.maximum(speed_x, speed_y))
    pseudo_step = 1.0 / (speed_x + speed_y + omega * (NT // 2))
    below = jnp.einsum('nm,mvi->nvi', lag_matrix(NT, sigma), state[:, :, -1], precision=lax.Precision.HIGHEST)
    above = jnp.einsum('nm,mvi->nvi', lag_matrix(NT, -sigma), state[:, :, 0], precision=lax.Precision.HIGHEST)

    def one_instance(packed):
        field, extra, step_size, lower_row, upper_row = packed
        current = field
        for weight in SEGMENT_WEIGHTS:
            padded = jnp.concatenate([lower_row[:, :, None], current, upper_row[:, :, None]], 2)
            current = field - weight * step_size[:, None] * (residual(padded, wave_max, wall_distance) + extra)
        return current - field
    packs = (state[:, None], source[:, None], pseudo_step[:, None], below[:, None], above[:, None])
    return lax.map(one_instance, packs)[:, 0]
```

```python
import functools
import math

import jax
import jax.numpy as jnp
from jax import lax
from jax.experimental import pallas as pl
from jax.experimental.pallas import tpu as pltpu
from jax.sharding import Mesh
from jax.sharding import PartitionSpec as P

NT = 16
HALF = NT // 2
ROTATION = 0.001
SEGMENT_WEIGHTS = (0.25, 1.0 / 6.0, 0.375, 0.5, 1.0)
CELLS = ("y", "zl", "core")
VMEM = pl.BlockSpec(memory_space=pltpu.VMEM)
SMEM = pl.BlockSpec(memory_space=pltpu.SMEM)
PARAMS = pltpu.CompilerParams(vmem_limit_bytes=48 * 1024 * 1024)

SLOPE = [
    -(2.0 / NT) * sum(k * math.sin(2.0 * math.pi * k * j / NT) for k in range(1, HALF))
    for j in range(NT)
]


def omega_of(counts_ref):
    return (2.0 * math.pi * ROTATION) * counts_ref[1].astype(jnp.float32)


def speed_sum_and_max(r, mx, my, e):
    inv = 1.0 / r
    vx = mx * inv
    vy = my * inv
    p = 0.4 * (e - 0.5 * (mx * vx + my * vy))
    c = jnp.sqrt(1.4 * p * inv)
    ax = jnp.abs(vx)
    ay = jnp.abs(vy)
    return ax + ay + 2.0 * c, jnp.maximum(ax, ay) + c


def peak_kernel(state_ref, out_ref):
    best = None
    for n in range(2):
        for t in range(2):
            rows = pl.ds(8 * t, 8)
            _, top = speed_sum_and_max(*(state_ref[n, v, rows, :] for v in range(4)))
            best = top if best is None else jnp.maximum(best, top)
    peak = jnp.max(best, axis=(0, 1), keepdims=True)
    out_ref[...] = jnp.broadcast_to(peak[None], out_ref.shape)


def partial_kernel(counts_ref, state_ref, other_ref, peaks_ref, out_ref, lag_ref):
    me_x = lax.axis_index("x")
    upper_half = lax.axis_index("zh")
    place = lax.axis_index(CELLS)
    is_last = place == lax.axis_size(CELLS) - 1
    omega = omega_of(counts_ref)
    ratio = jnp.full((NT, 128), counts_ref[1].astype(jnp.float32)) / jnp.full(
        (NT, 128), counts_ref[0].astype(jnp.float32)
    )
    sigma = 2.0 * math.pi * ratio
    shift = jnp.where(is_last, sigma, -sigma)
    offset = lax.broadcasted_iota(jnp.int32, (NT, 128), 0).astype(jnp.float32)
    order = lax.broadcasted_iota(jnp.int32, (NT, 128), 1)
    angle = (2.0 * math.pi / NT) * offset + shift
    share = jnp.where(order > HALF, 0.0, jnp.where((order == 0) | (order == HALF), 1.0, 2.0))
    terms = share * jnp.cos(order.astype(jnp.float32) * angle)
    lag_ref[...] = jnp.broadcast_to(
        jnp.sum(terms, axis=1, keepdims=True) * (1.0 / NT), lag_ref.shape
    )
    peak = jnp.max(peaks_ref[...], axis=0)
    for step in range(4):
        target = lax.rem(me_x + step, 4)
        own = [[(4 * step + n - m) % NT for m in range(2)] for n in range(2)]
        high = [[(4 * step + 2 + n - m) % NT for m in range(2)] for n in range(2)]
        low = [[(4 * step - 2 + n - m) % NT for m in range(2)] for n in range(2)]
        scale = [
            [omega * SLOPE[own[n][m]] for m in range(2)]
            + [
                omega * jnp.where(upper_half == 1, SLOPE[high[n][m]], SLOPE[low[n][m]])
                for m in range(2)
            ]
            for n in range(2)
        ]
        for v in range(5):
            for t in range(2):
                rows = pl.ds(8 * t, 8)
                fields = [state_ref[m, v, rows, :] for m in range(2)] + [
                    other_ref[m, v, rows, :] for m in range(2)
                ]
                for n in range(2):
                    total = scale[n][0] * fields[0]
                    for m in range(1, 4):
                        total = total + scale[n][m] * fields[m]
                    out_ref[target, pl.ds((n * 5 + v) * 16 + 8 * t, 8), :] = total

        def lag(j):
            return jnp.concatenate([lag_ref[j : j + 1, :]] * 4, axis=1)

        factor = [
            [lag(own[n][m]) for m in range(2)]
            + [jnp.where(upper_half == 1, lag(high[n][m]), lag(low[n][m])) for m in range(2)]
            for n in range(2)
        ]
        for v in range(5):
            edges = [
                jnp.where(is_last, ref[m, v, 15:16, :], ref[m, v, 0:1, :])
                for ref in (state_ref, other_ref)
                for m in range(2)
            ]
            for n in range(2):
                total = factor[n][0] * edges[0]
                for m in range(1, 4):
                    total = total + factor[n][m] * edges[m]
                out_ref[target, pl.ds(160 + n * 5 + v, 1), :] = total
        out_ref[target, pl.ds(170, 6), :] = jnp.broadcast_to(
            jnp.concatenate([peak] * 4, axis=1), (6, 512)
        )


def edge_kernel(state_ref, wall_ref, parts_ref, up_ref, down_ref):
    place = lax.axis_index(CELLS)
    is_first = place == 0
    is_last = place == lax.axis_size(CELLS) - 1
    row = lax.broadcasted_iota(jnp.int32, (8, 512), 0)

    def added(start, count):
        total = parts_ref[0, pl.ds(start, count), :]
        for k in range(1, 4):
            total = total + parts_ref[k, pl.ds(start, count), :]
        return total

    for n in range(2):
        for v in range(5):
            at = n * 5 + v
            lagged = jnp.broadcast_to(added(160 + at, 1), (8, 512))
            source = pltpu.roll(added(at * 16 + 8, 8), 4, axis=0)
            packed = jnp.where(row >= 4, state_ref[n, v, 8:16, :], source)
            packed = jnp.where(is_last & (row == 7), lagged, packed)
            up_ref[pl.ds(at * 8, 8), :] = packed
            source = pltpu.roll(added(at * 16, 8), 4, axis=0)
            packed = jnp.where(row < 4, state_ref[n, v, 0:8, :], source)
            packed = jnp.where(is_first & (row == 0), lagged, packed)
            down_ref[pl.ds(at * 8, 8), :] = packed
            up_ref[pl.ds(80 + at, 1), :] = state_ref[n, v, 11:12, :]
            down_ref[pl.ds(80 + at, 1), :] = state_ref[n, v, 4:5, :]
    up_ref[pl.ds(90, 4), :] = wall_ref[12:16, :]
    down_ref[pl.ds(90, 4), :] = wall_ref[0:4, :]
    peak = parts_ref[0, 170:172, :]
    for k in range(1, 4):
        peak = jnp.maximum(peak, parts_ref[k, 170:172, :])
    up_ref[pl.ds(94, 2), :] = peak
    down_ref[pl.ds(94, 2), :] = peak


def march_kernel(
    counts_ref,
    state_ref,
    wall_ref,
    parts_ref,
    lower_ref,
    upper_ref,
    out_ref,
    start_ref,
    now_ref,
    source_ref,
    step_ref,
    decay_ref,
    across_ref,
    ahead_ref,
    behind_ref,
):
    place = lax.axis_index(CELLS)
    is_first = place == 0
    is_last = place == lax.axis_size(CELLS) - 1
    omega = omega_of(counts_ref)
    row = lax.broadcasted_iota(jnp.int32, (8, 512), 0)
    column = lax.broadcasted_iota(jnp.int32, (8, 512), 1)
    at_left = column == 0
    at_right = column == 511
    peak = jnp.maximum(lower_ref[94:95, :], upper_ref[94:95, :])
    for k in range(4):
        peak = jnp.maximum(peak, parts_ref[k, 170:171, :])
    wave = jnp.broadcast_to(peak, (8, 512))

    walls = [
        jnp.concatenate([lower_ref[90:94, :]] * 2, axis=0),
        wall_ref[0:8, :],
        wall_ref[8:16, :],
        jnp.concatenate([upper_ref[90:94, :]] * 2, axis=0),
    ]
    for t in range(4):
        decay_ref[pl.ds(8 * t, 8), :] = 0.8 / (walls[t] * walls[t])
    for n in range(2):
        for v in range(5):
            at = n * 5 + v
            packed = lower_ref[pl.ds(at * 8, 8), :]
            fifth = jnp.broadcast_to(lower_ref[pl.ds(80 + at, 1), :], (8, 512))
            start_ref[n, v, 0:8, :] = jnp.where(row >= 4, packed, fifth)
            source_ref[n, v, 0:8, :] = 2.0 * pltpu.roll(packed, 4, axis=0)
            packed = upper_ref[pl.ds(at * 8, 8), :]
            fifth = jnp.broadcast_to(upper_ref[pl.ds(80 + at, 1), :], (8, 512))
            start_ref[n, v, 24:32, :] = jnp.where(row < 4, packed, fifth)
            source_ref[n, v, 24:32, :] = 2.0 * pltpu.roll(packed, 4, axis=0)
            start_ref[n, v, 8:24, :] = state_ref[n, v, :, :]
            total = parts_ref[0, pl.ds(at * 16, 16), :]
            for k in range(1, 4):
                total = total + parts_ref[k, pl.ds(at * 16, 16), :]
            source_ref[n, v, 8:24, :] = 2.0 * total
        for t in range(4):
            rows = pl.ds(8 * t, 8)
            both, _ = speed_sum_and_max(*(start_ref[n, v, rows, :] for v in range(4)))
            step_ref[n, rows, :] = 0.5 / (both + omega * HALF)

    for segment, weight in enumerate(SEGMENT_WEIGHTS):
        from_ref = start_ref if segment == 0 else now_ref
        for n in range(2):
            for t in range(4):
                rows = pl.ds(8 * t, 8)
                r, mx, my, e, q = (from_ref[n, v, rows, :] for v in range(5))
                inv = 1.0 / r
                vx = mx * inv
                vy = my * inv
                p = 0.4 * (e - 0.5 * (mx * vx + my * vy))
                h = e + p
                fx = (mx, mx * vx + p, my * vx, h * vx, q * vx)
                fy = (my, mx * vy, my * vy + p, h * vy, q * vy)
                for v, u in enumerate((r, mx, my, e, q)):
                    wu = wave * u
                    after = fx[v] - wu
                    before = fx[v] + wu
                    after = jnp.where(at_right, after, pltpu.roll(after, 511, axis=1))
                    before = jnp.where(at_left, before, pltpu.roll(before, 1, axis=1))
                    balance = after - before + 4.0 * wu
                    if v == 4:
                        balance = balance + decay_ref[rows, :] * (q * q * inv)
                    across_ref[v, rows, :] = balance
                    ahead_ref[v, pl.ds(8 * t + 8, 8), :] = fy[v] - wu
                    behind_ref[v, pl.ds(8 * t + 8, 8), :] = fy[v] + wu
            last = segment == len(SEGMENT_WEIGHTS) - 1
            for t in (1, 2) if last else range(4):
                rows = pl.ds(8 * t, 8)
                step = weight * step_ref[n, rows, :]
                for v in range(5):
                    total = (
                        across_ref[v, rows, :]
                        + ahead_ref[v, pl.ds(8 * t + 9, 8), :]
                        - behind_ref[v, pl.ds(8 * t + 7, 8), :]
                        + source_ref[n, v, rows, :]
                    )
                    change = step * total
                    begin = start_ref[n, v, rows, :]
                    if last:
                        out_ref[n, v, pl.ds(8 * t - 8, 8), :] = -change
                        continue
                    after = begin - change
                    if t == 0:
                        after = jnp.where(is_first, begin, after)
                    if t == 3:
                        after = jnp.where(is_last, begin, after)
                    now_ref[n, v, rows, :] = after


def local(state, wall_distance, blade_counts):
    f32 = jnp.float32
    field = functools.partial(jax.ShapeDtypeStruct, dtype=f32)
    other = lax.ppermute(state, "zh", [(0, 1), (1, 0)])
    peak = pl.pallas_call(
        peak_kernel, out_shape=field((128, 1, 128)), in_specs=[VMEM], out_specs=VMEM,
        compiler_params=PARAMS, name="peak",
    )(state)
    peaks = lax.all_to_all(peak, ("y", "zl", "zh"), 0, 0)
    parts = pl.pallas_call(
        partial_kernel, out_shape=field((4, 176, 512)),
        in_specs=[SMEM, VMEM, VMEM, VMEM], out_specs=VMEM,
        scratch_shapes=[pltpu.VMEM((NT, 128), f32)],
        compiler_params=PARAMS, name="partial_sources",
    )(blade_counts, state, other, peaks)
    parts = lax.all_to_all(parts, "x", 0, 0)
    up, down = pl.pallas_call(
        edge_kernel, out_shape=(field((96, 512)), field((96, 512))),
        in_specs=[VMEM] * 3, out_specs=(VMEM, VMEM),
        compiler_params=PARAMS, name="edges",
    )(state, wall_distance, parts)
    count = lax.axis_size(CELLS)
    ring = [(i, (i + 1) % count) for i in range(count)]
    lower = lax.ppermute(up, CELLS, ring)
    upper = lax.ppermute(down, CELLS, [(j, i) for i, j in ring])
    return pl.pallas_call(
        march_kernel, out_shape=field(state.shape),
        in_specs=[SMEM] + [VMEM] * 5, out_specs=VMEM,
        scratch_shapes=[
            pltpu.VMEM((2, 5, 32, 512), f32),
            pltpu.VMEM((2, 5, 32, 512), f32),
            pltpu.VMEM((2, 5, 32, 512), f32),
            pltpu.VMEM((2, 32, 512), f32),
            pltpu.VMEM((32, 512), f32),
            pltpu.VMEM((5, 32, 512), f32),
            pltpu.VMEM((5, 48, 512), f32),
            pltpu.VMEM((5, 48, 512), f32),
        ],
        compiler_params=PARAMS, name="march",
    )(blade_counts, state, wall_distance, parts, lower, upper)


def solution(mesh):
    fine = Mesh(mesh.devices.reshape(8, 8, 2, 4, 2), ("y", "zl", "core", "x", "zh"))
    inst = ("x", "zh")
    placed = (P(inst, None, CELLS, None), P(CELLS, None), P())
    return jax.shard_map(
        local, mesh=fine, in_specs=placed, out_specs=P(inst, None, CELLS, None), check_vma=False
    )
```

```python
import functools
import math

import jax
import jax.numpy as jnp
from jax import lax
from jax.experimental import pallas as pl
from jax.experimental.pallas import tpu as pltpu
from jax.sharding import Mesh
from jax.sharding import PartitionSpec as P

NT = 16
HALF = NT // 2
ROTATION = 0.001
SEGMENT_WEIGHTS = (0.25, 1.0 / 6.0, 0.375, 0.5, 1.0)
CELLS = ("y", "zl", "core")
VMEM = pl.BlockSpec(memory_space=pltpu.VMEM)
SMEM = pl.BlockSpec(memory_space=pltpu.SMEM)
PARAMS = pltpu.CompilerParams(vmem_limit_bytes=48 * 1024 * 1024)

SLOPE = [
    -(2.0 / NT) * sum(k * math.sin(2.0 * math.pi * k * j / NT) for k in range(1, HALF))
    for j in range(NT)
]


def omega_of(counts_ref):
    return (2.0 * math.pi * ROTATION) * counts_ref[1].astype(jnp.float32)


def speed_sum_and_max(r, mx, my, e):
    inv = 1.0 / r
    vx = mx * inv
    vy = my * inv
    p = 0.4 * (e - 0.5 * (mx * vx + my * vy))
    c = jnp.sqrt(1.4 * p * inv)
    ax = jnp.abs(vx)
    ay = jnp.abs(vy)
    return ax + ay + 2.0 * c, jnp.maximum(ax, ay) + c


def peak_kernel(state_ref, out_ref):
    best = None
    for n in range(2):
        for t in range(2):
            rows = pl.ds(8 * t, 8)
            _, top = speed_sum_and_max(*(state_ref[n, v, rows, :] for v in range(4)))
            best = top if best is None else jnp.maximum(best, top)
    peak = jnp.max(best, axis=(0, 1), keepdims=True)
    out_ref[...] = jnp.broadcast_to(peak[None], out_ref.shape)


def partial_kernel(counts_ref, state_ref, other_ref, peaks_ref, *rest):
    *out_refs, peak_ref, lag_ref = rest
    peak = jnp.max(peaks_ref[...], axis=0)
    peak_ref[...] = jnp.broadcast_to(peak[None], peak_ref.shape)
    upper_half = lax.axis_index("zh")
    place = lax.axis_index(CELLS)
    is_last = place == lax.axis_size(CELLS) - 1
    omega = omega_of(counts_ref)
    ratio = jnp.full((NT, 128), counts_ref[1].astype(jnp.float32)) / jnp.full(
        (NT, 128), counts_ref[0].astype(jnp.float32)
    )
    sigma = 2.0 * math.pi * ratio
    shift = jnp.where(is_last, sigma, -sigma)
    offset = lax.broadcasted_iota(jnp.int32, (NT, 128), 0).astype(jnp.float32)
    order = lax.broadcasted_iota(jnp.int32, (NT, 128), 1)
    angle = (2.0 * math.pi / NT) * offset + shift
    share = jnp.where(order > HALF, 0.0, jnp.where((order == 0) | (order == HALF), 1.0, 2.0))
    terms = share * jnp.cos(order.astype(jnp.float32) * angle)
    lag_ref[...] = jnp.broadcast_to(
        jnp.sum(terms, axis=1, keepdims=True) * (1.0 / NT), lag_ref.shape
    )
    for step, out_ref in enumerate(out_refs):
        own = [[(4 * step + n - m) % NT for m in range(2)] for n in range(2)]
        high = [[(4 * step + 2 + n - m) % NT for m in range(2)] for n in range(2)]
        low = [[(4 * step - 2 + n - m) % NT for m in range(2)] for n in range(2)]
        scale = [
            [omega * SLOPE[own[n][m]] for m in range(2)]
            + [
                omega * jnp.where(upper_half == 1, SLOPE[high[n][m]], SLOPE[low[n][m]])
                for m in range(2)
            ]
            for n in range(2)
        ]
        for v in range(5):
            for t in range(2):
                rows = pl.ds(8 * t, 8)
                fields = [state_ref[m, v, rows, :] for m in range(2)] + [
                    other_ref[m, v, rows, :] for m in range(2)
                ]
                for n in range(2):
                    total = scale[n][0] * fields[0]
                    for m in range(1, 4):
                        total = total + scale[n][m] * fields[m]
                    out_ref[pl.ds((n * 5 + v) * 16 + 8 * t, 8), :] = total

        def lag(j):
            return jnp.concatenate([lag_ref[j : j + 1, :]] * 4, axis=1)

        factor = [
            [lag(own[n][m]) for m in range(2)]
            + [jnp.where(upper_half == 1, lag(high[n][m]), lag(low[n][m])) for m in range(2)]
            for n in range(2)
        ]
        for v in range(5):
            edges = [
                jnp.where(is_last, ref[m, v, 15:16, :], ref[m, v, 0:1, :])
                for ref in (state_ref, other_ref)
                for m in range(2)
            ]
            for n in range(2):
                total = factor[n][0] * edges[0]
                for m in range(1, 4):
                    total = total + factor[n][m] * edges[m]
                out_ref[pl.ds(160 + n * 5 + v, 1), :] = total


def edge_kernel(state_ref, wall_ref, peaks_ref, part0, part1, part2, part3, far_ref, near_ref):
    place = lax.axis_index(CELLS)
    is_first = place == 0
    is_last = place == lax.axis_size(CELLS) - 1
    is_even = lax.axis_index("core") == 0
    row = lax.broadcasted_iota(jnp.int32, (8, 512), 0)

    def put(rows, up, down):
        far_ref[rows, :] = jnp.where(is_even, down, up)
        near_ref[rows, :] = jnp.where(is_even, up, down)

    def added(start, count):
        rows = pl.ds(start, count)
        return (part0[rows, :] + part1[rows, :]) + (part2[rows, :] + part3[rows, :])

    for n in range(2):
        for v in range(5):
            at = n * 5 + v
            lagged = jnp.broadcast_to(added(160 + at, 1), (8, 512))
            source = pltpu.roll(added(at * 16 + 8, 8), 4, axis=0)
            up = jnp.where(row >= 4, state_ref[n, v, 8:16, :], source)
            up = jnp.where(is_last & (row == 7), lagged, up)
            source = pltpu.roll(added(at * 16, 8), 4, axis=0)
            down = jnp.where(row < 4, state_ref[n, v, 0:8, :], source)
            down = jnp.where(is_first & (row == 0), lagged, down)
            put(pl.ds(at * 8, 8), up, down)
            put(pl.ds(80 + at, 1), state_ref[n, v, 11:12, :], state_ref[n, v, 4:5, :])
    put(pl.ds(90, 4), wall_ref[12:16, :], wall_ref[0:4, :])
    peak = jnp.max(peaks_ref[...], axis=0)
    peak = jnp.broadcast_to(jnp.concatenate([peak] * 4, axis=1), (2, 512))
    far_ref[94:96, :] = peak
    near_ref[94:96, :] = peak


def march_kernel(
    counts_ref,
    state_ref,
    wall_ref,
    part0,
    part1,
    part2,
    part3,
    far_ref,
    near_ref,
    peaks_ref,
    out_ref,
    start_ref,
    now_ref,
    source_ref,
    step_ref,
    decay_ref,
    across_ref,
    ahead_ref,
    behind_ref,
):
    place = lax.axis_index(CELLS)
    is_first = place == 0
    is_last = place == lax.axis_size(CELLS) - 1
    omega = omega_of(counts_ref)
    row = lax.broadcasted_iota(jnp.int32, (8, 512), 0)
    column = lax.broadcasted_iota(jnp.int32, (8, 512), 1)
    at_left = column == 0
    at_right = column == 511
    is_even = lax.axis_index("core") == 0

    def lower(rows):
        return jnp.where(is_even, far_ref[rows, :], near_ref[rows, :])

    def upper(rows):
        return jnp.where(is_even, near_ref[rows, :], far_ref[rows, :])

    peak = jnp.max(peaks_ref[...], axis=0)
    peak = jnp.concatenate([peak] * 4, axis=1)
    peak = jnp.maximum(peak, near_ref[94:95, :])
    wave = jnp.broadcast_to(peak, (8, 512))

    walls = [
        jnp.concatenate([lower(pl.ds(90, 4))] * 2, axis=0),
        wall_ref[0:8, :],
        wall_ref[8:16, :],
        jnp.concatenate([upper(pl.ds(90, 4))] * 2, axis=0),
    ]
    for t in range(4):
        decay_ref[pl.ds(8 * t, 8), :] = 0.8 / (walls[t] * walls[t])
    for n in range(2):
        for v in range(5):
            at = n * 5 + v
            packed = lower(pl.ds(at * 8, 8))
            fifth = jnp.broadcast_to(lower(pl.ds(80 + at, 1)), (8, 512))
            start_ref[n, v, 0:8, :] = jnp.where(row >= 4, packed, fifth)
            source_ref[n, v, 0:8, :] = 2.0 * pltpu.roll(packed, 4, axis=0)
            packed = upper(pl.ds(at * 8, 8))
            fifth = jnp.broadcast_to(upper(pl.ds(80 + at, 1)), (8, 512))
            start_ref[n, v, 24:32, :] = jnp.where(row < 4, packed, fifth)
            source_ref[n, v, 24:32, :] = 2.0 * pltpu.roll(packed, 4, axis=0)
            start_ref[n, v, 8:24, :] = state_ref[n, v, :, :]
            rows = pl.ds(at * 16, 16)
            total = (part0[rows, :] + part1[rows, :]) + (part2[rows, :] + part3[rows, :])
            source_ref[n, v, 8:24, :] = 2.0 * total
        for t in range(4):
            rows = pl.ds(8 * t, 8)
            both, _ = speed_sum_and_max(*(start_ref[n, v, rows, :] for v in range(4)))
            step_ref[n, rows, :] = 0.5 / (both + omega * HALF)

    for segment, weight in enumerate(SEGMENT_WEIGHTS):
        from_ref = start_ref if segment == 0 else now_ref
        for n in range(2):
            for t in range(4):
                rows = pl.ds(8 * t, 8)
                r, mx, my, e, q = (from_ref[n, v, rows, :] for v in range(5))
                inv = 1.0 / r
                vx = mx * inv
                vy = my * inv
                p = 0.4 * (e - 0.5 * (mx * vx + my * vy))
                h = e + p
                fx = (mx, mx * vx + p, my * vx, h * vx, q * vx)
                fy = (my, mx * vy, my * vy + p, h * vy, q * vy)
                for v, u in enumerate((r, mx, my, e, q)):
                    wu = wave * u
                    after = fx[v] - wu
                    before = fx[v] + wu
                    after = jnp.where(at_right, after, pltpu.roll(after, 511, axis=1))
                    before = jnp.where(at_left, before, pltpu.roll(before, 1, axis=1))
                    balance = after - before + 4.0 * wu
                    if v == 4:
                        balance = balance + decay_ref[rows, :] * (q * q * inv)
                    across_ref[v, rows, :] = balance
                    ahead_ref[v, pl.ds(8 * t + 8, 8), :] = fy[v] - wu
                    behind_ref[v, pl.ds(8 * t + 8, 8), :] = fy[v] + wu
            last = segment == len(SEGMENT_WEIGHTS) - 1
            for t in (1, 2) if last else range(4):
                rows = pl.ds(8 * t, 8)
                step = weight * step_ref[n, rows, :]
                for v in range(5):
                    total = (
                        across_ref[v, rows, :]
                        + ahead_ref[v, pl.ds(8 * t + 9, 8), :]
                        - behind_ref[v, pl.ds(8 * t + 7, 8), :]
                        + source_ref[n, v, rows, :]
                    )
                    change = step * total
                    begin = start_ref[n, v, rows, :]
                    if last:
                        out_ref[n, v, pl.ds(8 * t - 8, 8), :] = -change
                        continue
                    after = begin - change
                    if t == 0:
                        after = jnp.where(is_first, begin, after)
                    if t == 3:
                        after = jnp.where(is_last, begin, after)
                    now_ref[n, v, rows, :] = after


def local(state, wall_distance, blade_counts):
    f32 = jnp.float32
    field = functools.partial(jax.ShapeDtypeStruct, dtype=f32)
    other = lax.ppermute(state, "zh", [(0, 1), (1, 0)])
    peak = pl.pallas_call(
        peak_kernel, out_shape=field((32, 1, 128)), in_specs=[VMEM], out_specs=VMEM,
        compiler_params=PARAMS, name="peak",
    )(state)
    peaks = lax.all_to_all(peak, ("y", "x"), 0, 0)
    *parts, peak = pl.pallas_call(
        partial_kernel, out_shape=[field((176, 512))] * 4 + [field((16, 1, 128))],
        in_specs=[SMEM, VMEM, VMEM, VMEM], out_specs=[VMEM] * 5,
        scratch_shapes=[pltpu.VMEM((NT, 128), f32)],
        compiler_params=PARAMS, name="partial_sources",
    )(blade_counts, state, other, peaks)
    sent = [
        lax.ppermute(parts[step], "x", [(i, (i + step) % 4) for i in range(4)])
        for step in (2, 1, 3)
    ]
    parts = [parts[0], *sent]
    peaks = lax.all_to_all(peak, ("zl", "zh"), 0, 0)
    far, near = pl.pallas_call(
        edge_kernel, out_shape=(field((96, 512)), field((96, 512))),
        in_specs=[VMEM] * 7, out_specs=(VMEM, VMEM),
        compiler_params=PARAMS, name="edges",
    )(state, wall_distance, peaks, *parts)
    count = lax.axis_size(CELLS)
    across = [((i + 1) % count, (i + 2) % count) for i in range(0, count, 2)]
    far = lax.ppermute(far, CELLS, across + [(j, i) for i, j in across])
    near = lax.ppermute(near, "core", [(0, 1), (1, 0)])
    return pl.pallas_call(
        march_kernel, out_shape=field(state.shape),
        in_specs=[SMEM] + [VMEM] * 9, out_specs=VMEM,
        scratch_shapes=[
            pltpu.VMEM((2, 5, 32, 512), f32),
            pltpu.VMEM((2, 5, 32, 512), f32),
            pltpu.VMEM((2, 5, 32, 512), f32),
            pltpu.VMEM((2, 32, 512), f32),
            pltpu.VMEM((32, 512), f32),
            pltpu.VMEM((5, 32, 512), f32),
            pltpu.VMEM((5, 48, 512), f32),
            pltpu.VMEM((5, 48, 512), f32),
        ],
        compiler_params=PARAMS, name="march",
    )(blade_counts, state, wall_distance, *parts, far, near, peaks)


def solution(mesh):
    fine = Mesh(mesh.devices.reshape(8, 8, 2, 4, 2), ("y", "zl", "core", "x", "zh"))
    inst = ("x", "zh")
    placed = (P(inst, None, CELLS, None), P(CELLS, None), P())
    return jax.shard_map(
        local, mesh=fine, in_specs=placed, out_specs=P(inst, None, CELLS, None), check_vma=False
    )
```

```python
import functools
import math

import jax
import jax.numpy as jnp
from jax import lax
from jax.experimental import pallas as pl
from jax.experimental.pallas import tpu as pltpu
from jax.sharding import Mesh
from jax.sharding import PartitionSpec as P

NT = 16
HALF = NT // 2
ROTATION = 0.001
SEGMENT_WEIGHTS = (0.25, 1.0 / 6.0, 0.375, 0.5, 1.0)
CELLS = ("y", "zl", "core")
VMEM = pl.BlockSpec(memory_space=pltpu.VMEM)
SMEM = pl.BlockSpec(memory_space=pltpu.SMEM)
PARAMS = pltpu.CompilerParams(vmem_limit_bytes=12 * 1024 * 1024)

SLOPE = [
    -(2.0 / NT) * sum(k * math.sin(2.0 * math.pi * k * j / NT) for k in range(1, HALF))
    for j in range(NT)
]


def omega_of(counts_ref):
    return (2.0 * math.pi * ROTATION) * counts_ref[1]


def speed_sum_and_max(r, mx, my, e):
    inv = 1.0 / r
    vx = mx * inv
    vy = my * inv
    p = 0.4 * (e - 0.5 * (mx * vx + my * vy))
    c = jnp.sqrt(1.4 * p * inv)
    ax = jnp.abs(vx)
    ay = jnp.abs(vy)
    return ax + ay + 2.0 * c, jnp.maximum(ax, ay) + c


def peak_kernel(whole_ref, state_ref, out_ref, counts_ref, held_ref):
    held_ref[...] = state_ref[...]
    for k in range(2):
        counts_ref[k] = whole_ref[k].astype(jnp.float32)
    best = None
    for n in range(2):
        for t in range(2):
            rows = pl.ds(8 * t, 8)
            _, top = speed_sum_and_max(*(state_ref[n, v, rows, :] for v in range(4)))
            best = top if best is None else jnp.maximum(best, top)
    peak = jnp.max(best, axis=(0, 1), keepdims=True)
    out_ref[...] = jnp.broadcast_to(peak[None], out_ref.shape)


def fold_kernel(peaks_ref, out_ref):
    peak = jnp.max(peaks_ref[...], axis=0)
    out_ref[...] = jnp.broadcast_to(peak[None], out_ref.shape)


def partial_kernel(counts_ref, state_ref, other_ref, peaks_ref, out_ref, lag_ref):
    me_x = lax.axis_index("x")
    peak = jnp.max(peaks_ref[...], axis=0)
    upper_half = lax.axis_index("zh")
    place = lax.axis_index(CELLS)
    is_last = place == lax.axis_size(CELLS) - 1
    omega = omega_of(counts_ref)
    ratio = jnp.full((NT, 128), counts_ref[1]) / jnp.full((NT, 128), counts_ref[0])
    sigma = 2.0 * math.pi * ratio
    shift = jnp.where(is_last, sigma, -sigma)
    offset = lax.broadcasted_iota(jnp.int32, (NT, 128), 0).astype(jnp.float32)
    order = lax.broadcasted_iota(jnp.int32, (NT, 128), 1)
    angle = (2.0 * math.pi / NT) * offset + shift
    share = jnp.where(order > HALF, 0.0, jnp.where((order == 0) | (order == HALF), 1.0, 2.0))
    terms = share * jnp.cos(order.astype(jnp.float32) * angle)
    lag_ref[...] = jnp.broadcast_to(
        jnp.sum(terms, axis=1, keepdims=True) * (1.0 / NT), lag_ref.shape
    )
    for step in range(4):
        target = lax.rem(me_x + step, 4)
        own = [[(4 * step + n - m) % NT for m in range(2)] for n in range(2)]
        high = [[(4 * step + 2 + n - m) % NT for m in range(2)] for n in range(2)]
        low = [[(4 * step - 2 + n - m) % NT for m in range(2)] for n in range(2)]
        scale = [
            [omega * SLOPE[own[n][m]] for m in range(2)]
            + [
                omega * jnp.where(upper_half == 1, SLOPE[high[n][m]], SLOPE[low[n][m]])
                for m in range(2)
            ]
            for n in range(2)
        ]
        for v in range(5):
            for t in range(2):
                rows = pl.ds(8 * t, 8)
                fields = [state_ref[m, v, rows, :] for m in range(2)] + [
                    other_ref[m, v, rows, :] for m in range(2)
                ]
                for n in range(2):
                    total = scale[n][0] * fields[0]
                    for m in range(1, 4):
                        total = total + scale[n][m] * fields[m]
                    out_ref[target, pl.ds((n * 5 + v) * 16 + 8 * t, 8), :] = total

        def lag(j):
            return jnp.concatenate([lag_ref[j : j + 1, :]] * 4, axis=1)

        factor = [
            [lag(own[n][m]) for m in range(2)]
            + [jnp.where(upper_half == 1, lag(high[n][m]), lag(low[n][m])) for m in range(2)]
            for n in range(2)
        ]
        for v in range(5):
            edges = [
                jnp.where(is_last, ref[m, v, 15:16, :], ref[m, v, 0:1, :])
                for ref in (state_ref, other_ref)
                for m in range(2)
            ]
            for n in range(2):
                total = factor[n][0] * edges[0]
                for m in range(1, 4):
                    total = total + factor[n][m] * edges[m]
                out_ref[target, pl.ds(160 + n * 5 + v, 1), :] = total
        out_ref[target, pl.ds(170, 6), :] = jnp.broadcast_to(
            jnp.concatenate([peak] * 4, axis=1), (6, 512)
        )


def edge_kernel(state_ref, wall_ref, parts_ref, far_ref, near_ref):
    place = lax.axis_index(CELLS)
    is_first = place == 0
    is_last = place == lax.axis_size(CELLS) - 1
    is_even = lax.axis_index("core") == 0
    row = lax.broadcasted_iota(jnp.int32, (8, 512), 0)

    def put(rows, up, down):
        far_ref[rows, :] = jnp.where(is_even, down, up)
        near_ref[rows, :] = jnp.where(is_even, up, down)

    def added(start, count):
        rows = pl.ds(start, count)
        return (parts_ref[0, rows, :] + parts_ref[1, rows, :]) + (
            parts_ref[2, rows, :] + parts_ref[3, rows, :]
        )

    for n in range(2):
        for v in range(5):
            at = n * 5 + v
            lagged = jnp.broadcast_to(added(160 + at, 1), (8, 512))
            source = pltpu.roll(added(at * 16 + 8, 8), 4, axis=0)
            up = jnp.where(row >= 4, state_ref[n, v, 8:16, :], source)
            up = jnp.where(is_last & (row == 7), lagged, up)
            source = pltpu.roll(added(at * 16, 8), 4, axis=0)
            down = jnp.where(row < 4, state_ref[n, v, 0:8, :], source)
            down = jnp.where(is_first & (row == 0), lagged, down)
            put(pl.ds(at * 8, 8), up, down)
            put(pl.ds(80 + at, 1), state_ref[n, v, 11:12, :], state_ref[n, v, 4:5, :])
    put(pl.ds(90, 4), wall_ref[12:16, :], wall_ref[0:4, :])
    put(pl.ds(94, 2), wall_ref[14:16, :], wall_ref[0:2, :])


def march_kernel(
    counts_ref,
    state_ref,
    wall_ref,
    parts_ref,
    far_ref,
    near_ref,
    out_ref,
    start_ref,
    now_ref,
    source_ref,
    step_ref,
    decay_ref,
    across_ref,
    ahead_ref,
    behind_ref,
):
    place = lax.axis_index(CELLS)
    is_first = place == 0
    is_last = place == lax.axis_size(CELLS) - 1
    omega = omega_of(counts_ref)
    row = lax.broadcasted_iota(jnp.int32, (8, 512), 0)
    column = lax.broadcasted_iota(jnp.int32, (8, 512), 1)
    at_left = column == 0
    at_right = column == 511
    is_even = lax.axis_index("core") == 0

    def lower(rows):
        return jnp.where(is_even, far_ref[rows, :], near_ref[rows, :])

    def upper(rows):
        return jnp.where(is_even, near_ref[rows, :], far_ref[rows, :])

    peak = parts_ref[0, 170:171, :]
    for k in range(1, 4):
        peak = jnp.maximum(peak, parts_ref[k, 170:171, :])
    wave = jnp.broadcast_to(peak, (8, 512))

    walls = [
        jnp.concatenate([lower(pl.ds(90, 4))] * 2, axis=0),
        wall_ref[0:8, :],
        wall_ref[8:16, :],
        jnp.concatenate([upper(pl.ds(90, 4))] * 2, axis=0),
    ]
    for t in range(4):
        decay_ref[pl.ds(8 * t, 8), :] = 0.8 / (walls[t] * walls[t])
    for n in range(2):
        for v in range(5):
            at = n * 5 + v
            packed = lower(pl.ds(at * 8, 8))
            fifth = jnp.broadcast_to(lower(pl.ds(80 + at, 1)), (8, 512))
            start_ref[n, v, 0:8, :] = jnp.where(row >= 4, packed, fifth)
            source_ref[n, v, 0:8, :] = 2.0 * pltpu.roll(packed, 4, axis=0)
            packed = upper(pl.ds(at * 8, 8))
            fifth = jnp.broadcast_to(upper(pl.ds(80 + at, 1)), (8, 512))
            start_ref[n, v, 24:32, :] = jnp.where(row < 4, packed, fifth)
            source_ref[n, v, 24:32, :] = 2.0 * pltpu.roll(packed, 4, axis=0)
            start_ref[n, v, 8:24, :] = state_ref[n, v, :, :]
            rows = pl.ds(at * 16, 16)
            total = (parts_ref[0, rows, :] + parts_ref[1, rows, :]) + (
                parts_ref[2, rows, :] + parts_ref[3, rows, :]
            )
            source_ref[n, v, 8:24, :] = 2.0 * total
        for t in range(4):
            rows = pl.ds(8 * t, 8)
            both, _ = speed_sum_and_max(*(start_ref[n, v, rows, :] for v in range(4)))
            step_ref[n, rows, :] = 0.5 / (both + omega * HALF)

    for segment, weight in enumerate(SEGMENT_WEIGHTS):
        from_ref = start_ref if segment == 0 else now_ref
        for n in range(2):
            for t in range(4):
                rows = pl.ds(8 * t, 8)
                r, mx, my, e, q = (from_ref[n, v, rows, :] for v in range(5))
                inv = 1.0 / r
                vx = mx * inv
                vy = my * inv
                p = 0.4 * (e - 0.5 * (mx * vx + my * vy))
                h = e + p
                fx = (mx, mx * vx + p, my * vx, h * vx, q * vx)
                fy = (my, mx * vy, my * vy + p, h * vy, q * vy)
                for v, u in enumerate((r, mx, my, e, q)):
                    wu = wave * u
                    after = fx[v] - wu
                    before = fx[v] + wu
                    after = jnp.where(at_right, after, pltpu.roll(after, 511, axis=1))
                    before = jnp.where(at_left, before, pltpu.roll(before, 1, axis=1))
                    balance = after - before + 4.0 * wu
                    if v == 4:
                        balance = balance + decay_ref[rows, :] * (q * q * inv)
                    across_ref[v, rows, :] = balance
                    ahead_ref[v, pl.ds(8 * t + 8, 8), :] = fy[v] - wu
                    behind_ref[v, pl.ds(8 * t + 8, 8), :] = fy[v] + wu
            last = segment == len(SEGMENT_WEIGHTS) - 1
            for t in (1, 2) if last else range(4):
                rows = pl.ds(8 * t, 8)
                step = weight * step_ref[n, rows, :]
                for v in range(5):
                    total = (
                        across_ref[v, rows, :]
                        + ahead_ref[v, pl.ds(8 * t + 9, 8), :]
                        - behind_ref[v, pl.ds(8 * t + 7, 8), :]
                        + source_ref[n, v, rows, :]
                    )
                    change = step * total
                    begin = start_ref[n, v, rows, :]
                    if last:
                        out_ref[n, v, pl.ds(8 * t - 8, 8), :] = -change
                        continue
                    after = begin - change
                    if t == 0:
                        after = jnp.where(is_first, begin, after)
                    if t == 3:
                        after = jnp.where(is_last, begin, after)
                    now_ref[n, v, rows, :] = after


def local(state, wall_distance, blade_counts):
    f32 = jnp.float32
    field = functools.partial(jax.ShapeDtypeStruct, dtype=f32)
    other = lax.ppermute(state, "zh", [(0, 1), (1, 0)])
    peak, counts, state = pl.pallas_call(
        peak_kernel, out_shape=(field((8, 1, 128)), field((2,)), field(state.shape)),
        in_specs=[SMEM, VMEM], out_specs=(VMEM, SMEM, VMEM),
        compiler_params=PARAMS, name="peak",
    )(blade_counts, state)
    peaks = lax.all_to_all(peak, "y", 0, 0)
    peak = pl.pallas_call(
        fold_kernel, out_shape=field((32, 1, 128)), in_specs=[VMEM], out_specs=VMEM,
        compiler_params=PARAMS, name="fold",
    )(peaks)
    peaks = lax.all_to_all(peak, ("zl", "zh", "core"), 0, 0)
    parts = pl.pallas_call(
        partial_kernel, out_shape=field((4, 176, 512)),
        in_specs=[SMEM, VMEM, VMEM, VMEM], out_specs=VMEM,
        scratch_shapes=[pltpu.VMEM((NT, 128), f32)],
        compiler_params=PARAMS, name="partial_sources",
    )(counts, state, other, peaks)
    parts = lax.all_to_all(parts, "x", 0, 0)
    far, near = pl.pallas_call(
        edge_kernel, out_shape=(field((96, 512)), field((96, 512))),
        in_specs=[VMEM] * 3, out_specs=(VMEM, VMEM),
        compiler_params=PARAMS, name="edges",
    )(state, wall_distance, parts)
    count = lax.axis_size(CELLS)
    across = [((i + 1) % count, (i + 2) % count) for i in range(0, count, 2)]
    far = lax.ppermute(far, CELLS, across + [(j, i) for i, j in across])
    near = lax.ppermute(near, "core", [(0, 1), (1, 0)])
    return pl.pallas_call(
        march_kernel, out_shape=field(state.shape),
        in_specs=[SMEM] + [VMEM] * 5, out_specs=VMEM,
        scratch_shapes=[
            pltpu.VMEM((2, 5, 32, 512), f32),
            pltpu.VMEM((2, 5, 32, 512), f32),
            pltpu.VMEM((2, 5, 32, 512), f32),
            pltpu.VMEM((2, 32, 512), f32),
            pltpu.VMEM((32, 512), f32),
            pltpu.VMEM((5, 32, 512), f32),
            pltpu.VMEM((5, 48, 512), f32),
            pltpu.VMEM((5, 48, 512), f32),
        ],
        compiler_params=PARAMS, name="march",
    )(counts, state, wall_distance, parts, far, near)


def solution(mesh):
    fine = Mesh(mesh.devices.reshape(8, 8, 2, 4, 2), ("y", "zl", "core", "x", "zh"))
    inst = ("x", "zh")
    placed = (P(inst, None, CELLS, None), P(CELLS, None), P())
    return jax.shard_map(
        local, mesh=fine, in_specs=placed, out_specs=P(inst, None, CELLS, None), check_vma=False
    )
```

```python
import functools
import math

import jax
import jax.numpy as jnp
from jax import lax
from jax.experimental import pallas as pl
from jax.experimental.pallas import tpu as pltpu
from jax.sharding import Mesh
from jax.sharding import PartitionSpec as P

NT = 16
HALF = NT // 2
ROTATION = 0.001
SEGMENT_WEIGHTS = (0.25, 1.0 / 6.0, 0.375, 0.5, 1.0)
CELLS = ("y", "zl", "core")
VMEM = pl.BlockSpec(memory_space=pltpu.VMEM)
SMEM = pl.BlockSpec(memory_space=pltpu.SMEM)
PARAMS = pltpu.CompilerParams(vmem_limit_bytes=12 * 1024 * 1024)

SLOPE = [
    -(2.0 / NT) * sum(k * math.sin(2.0 * math.pi * k * j / NT) for k in range(1, HALF))
    for j in range(NT)
]


def omega_of(counts_ref):
    return (2.0 * math.pi * ROTATION) * counts_ref[1]


def speed_sum_and_max(r, mx, my, e):
    inv = 1.0 / r
    vx = mx * inv
    vy = my * inv
    p = 0.4 * (e - 0.5 * (mx * vx + my * vy))
    c = jnp.sqrt(1.4 * p * inv)
    ax = jnp.abs(vx)
    ay = jnp.abs(vy)
    return ax + ay + 2.0 * c, jnp.maximum(ax, ay) + c


def peak_kernel(whole_ref, state_ref, out_ref, counts_ref, held_ref):
    held_ref[...] = state_ref[...]
    for k in range(2):
        counts_ref[k] = whole_ref[k].astype(jnp.float32)
    best = None
    for n in range(2):
        for t in range(2):
            rows = pl.ds(8 * t, 8)
            _, top = speed_sum_and_max(*(state_ref[n, v, rows, :] for v in range(4)))
            best = top if best is None else jnp.maximum(best, top)
    peak = jnp.max(best, axis=(0, 1), keepdims=True)
    out_ref[...] = jnp.broadcast_to(peak[None], out_ref.shape)


def fold_kernel(peaks_ref, out_ref):
    peak = jnp.max(peaks_ref[...], axis=0)
    out_ref[...] = jnp.broadcast_to(peak[None], out_ref.shape)


def add_partials(counts_ref, state_ref, other_ref, out_ref, edge):
    me_x = lax.axis_index("x")
    upper_half = lax.axis_index("zh")
    omega = omega_of(counts_ref)
    row = lax.broadcasted_iota(jnp.int32, (8, 512), 0)
    for v in range(5):
        fields = [
            jnp.where((row < 4) == edge, ref[m, v, 0:8, :], ref[m, v, 8:16, :])
            for ref in (state_ref, other_ref)
            for m in range(2)
        ]
        for step in range(4):
            target = lax.rem(me_x + step, 4)
            for n in range(2):
                total = None
                for m, field in enumerate(fields):
                    own, high, low = offsets(step, n, m)
                    factor = SLOPE[own]
                    if m >= 2:
                        factor = jnp.where(upper_half == 1, SLOPE[high], SLOPE[low])
                    term = (omega * factor) * field
                    total = term if total is None else total + term
                out_ref[target, pl.ds((n * 5 + v) * 8, 8), :] = total


def offsets(step, n, m):
    apart = 4 * step + n - m % 2
    return apart % NT, (apart + 2) % NT, (apart - 2) % NT


def partial_kernel(counts_ref, state_ref, other_ref, peaks_ref, out_ref, lag_ref):
    me_x = lax.axis_index("x")
    upper_half = lax.axis_index("zh")
    place = lax.axis_index(CELLS)
    is_last = place == lax.axis_size(CELLS) - 1
    add_partials(counts_ref, state_ref, other_ref, out_ref, True)
    ratio = jnp.full((NT, 128), counts_ref[1]) / jnp.full((NT, 128), counts_ref[0])
    sigma = 2.0 * math.pi * ratio
    shift = jnp.where(is_last, sigma, -sigma)
    offset = lax.broadcasted_iota(jnp.int32, (NT, 128), 0).astype(jnp.float32)
    order = lax.broadcasted_iota(jnp.int32, (NT, 128), 1)
    angle = (2.0 * math.pi / NT) * offset + shift
    share = jnp.where(order > HALF, 0.0, jnp.where((order == 0) | (order == HALF), 1.0, 2.0))
    terms = share * jnp.cos(order.astype(jnp.float32) * angle)
    lag_ref[...] = jnp.broadcast_to(
        jnp.sum(terms, axis=1, keepdims=True) * (1.0 / NT), lag_ref.shape
    )

    def lag(j):
        return jnp.concatenate([lag_ref[j : j + 1, :]] * 4, axis=1)

    peak = jnp.max(peaks_ref[...], axis=0)
    peak = jnp.broadcast_to(jnp.concatenate([peak] * 4, axis=1), (6, 512))
    for step in range(4):
        target = lax.rem(me_x + step, 4)
        for n in range(2):
            factor = []
            for m in range(4):
                own, high, low = offsets(step, n, m)
                factor.append(
                    lag(own) if m < 2 else jnp.where(upper_half == 1, lag(high), lag(low))
                )
            for v in range(5):
                total = None
                for m, ref in enumerate((state_ref, state_ref, other_ref, other_ref)):
                    edge = jnp.where(is_last, ref[m % 2, v, 15:16, :], ref[m % 2, v, 0:1, :])
                    term = factor[m] * edge
                    total = term if total is None else total + term
                out_ref[target, pl.ds(80 + n * 5 + v, 1), :] = total
        out_ref[target, pl.ds(90, 6), :] = peak


def added(parts_ref, start, count):
    rows = pl.ds(start, count)
    return (parts_ref[0, rows, :] + parts_ref[1, rows, :]) + (
        parts_ref[2, rows, :] + parts_ref[3, rows, :]
    )


def edge_kernel(counts_ref, state_ref, other_ref, wall_ref, outer_ref, far_ref, near_ref, inner_ref):
    place = lax.axis_index(CELLS)
    is_first = place == 0
    is_last = place == lax.axis_size(CELLS) - 1
    is_even = lax.axis_index("core") == 0
    row = lax.broadcasted_iota(jnp.int32, (8, 512), 0)

    def put(rows, up, down):
        far_ref[rows, :] = jnp.where(is_even, down, up)
        near_ref[rows, :] = jnp.where(is_even, up, down)

    for n in range(2):
        for v in range(5):
            at = n * 5 + v
            lagged = jnp.broadcast_to(added(outer_ref, 80 + at, 1), (8, 512))
            source = pltpu.roll(added(outer_ref, at * 8, 8), 4, axis=0)
            up = jnp.where(row >= 4, state_ref[n, v, 8:16, :], source)
            up = jnp.where(is_last & (row == 7), lagged, up)
            down = jnp.where(row < 4, state_ref[n, v, 0:8, :], source)
            down = jnp.where(is_first & (row == 0), lagged, down)
            put(pl.ds(at * 8, 8), up, down)
            put(pl.ds(80 + at, 1), state_ref[n, v, 11:12, :], state_ref[n, v, 4:5, :])
    put(pl.ds(90, 4), wall_ref[12:16, :], wall_ref[0:4, :])
    put(pl.ds(94, 2), wall_ref[14:16, :], wall_ref[0:2, :])
    add_partials(counts_ref, state_ref, other_ref, inner_ref, False)


def march_kernel(
    counts_ref,
    state_ref,
    wall_ref,
    outer_ref,
    inner_ref,
    far_ref,
    near_ref,
    out_ref,
    start_ref,
    now_ref,
    source_ref,
    step_ref,
    decay_ref,
    across_ref,
    ahead_ref,
    behind_ref,
):
    place = lax.axis_index(CELLS)
    is_first = place == 0
    is_last = place == lax.axis_size(CELLS) - 1
    omega = omega_of(counts_ref)
    row = lax.broadcasted_iota(jnp.int32, (8, 512), 0)
    column = lax.broadcasted_iota(jnp.int32, (8, 512), 1)
    at_left = column == 0
    at_right = column == 511
    is_even = lax.axis_index("core") == 0

    def lower(rows):
        return jnp.where(is_even, far_ref[rows, :], near_ref[rows, :])

    def upper(rows):
        return jnp.where(is_even, near_ref[rows, :], far_ref[rows, :])

    peak = outer_ref[0, 90:91, :]
    for k in range(1, 4):
        peak = jnp.maximum(peak, outer_ref[k, 90:91, :])
    wave = jnp.broadcast_to(peak, (8, 512))

    walls = [
        jnp.concatenate([lower(pl.ds(90, 4))] * 2, axis=0),
        wall_ref[0:8, :],
        wall_ref[8:16, :],
        jnp.concatenate([upper(pl.ds(90, 4))] * 2, axis=0),
    ]
    for t in range(4):
        decay_ref[pl.ds(8 * t, 8), :] = 0.8 / (walls[t] * walls[t])
    for n in range(2):
        for v in range(5):
            at = n * 5 + v
            packed = lower(pl.ds(at * 8, 8))
            fifth = jnp.broadcast_to(lower(pl.ds(80 + at, 1)), (8, 512))
            start_ref[n, v, 0:8, :] = jnp.where(row >= 4, packed, fifth)
            source_ref[n, v, 0:8, :] = 2.0 * pltpu.roll(packed, 4, axis=0)
            packed = upper(pl.ds(at * 8, 8))
            fifth = jnp.broadcast_to(upper(pl.ds(80 + at, 1)), (8, 512))
            start_ref[n, v, 24:32, :] = jnp.where(row < 4, packed, fifth)
            source_ref[n, v, 24:32, :] = 2.0 * pltpu.roll(packed, 4, axis=0)
            start_ref[n, v, 8:24, :] = state_ref[n, v, :, :]
            outer = 2.0 * added(outer_ref, at * 8, 8)
            inner = 2.0 * added(inner_ref, at * 8, 8)
            source_ref[n, v, 8:16, :] = jnp.where(row < 4, outer, inner)
            source_ref[n, v, 16:24, :] = jnp.where(row < 4, inner, outer)
        for t in range(4):
            rows = pl.ds(8 * t, 8)
            both, _ = speed_sum_and_max(*(start_ref[n, v, rows, :] for v in range(4)))
            step_ref[n, rows, :] = 0.5 / (both + omega * HALF)

    for segment, weight in enumerate(SEGMENT_WEIGHTS):
        from_ref = start_ref if segment == 0 else now_ref
        for n in range(2):
            for t in range(4):
                rows = pl.ds(8 * t, 8)
                r, mx, my, e, q = (from_ref[n, v, rows, :] for v in range(5))
                inv = 1.0 / r
                vx = mx * inv
                vy = my * inv
                p = 0.4 * (e - 0.5 * (mx * vx + my * vy))
                h = e + p
                fx = (mx, mx * vx + p, my * vx, h * vx, q * vx)
                fy = (my, mx * vy, my * vy + p, h * vy, q * vy)
                for v, u in enumerate((r, mx, my, e, q)):
                    wu = wave * u
                    after = fx[v] - wu
                    before = fx[v] + wu
                    after = jnp.where(at_right, after, pltpu.roll(after, 511, axis=1))
                    before = jnp.where(at_left, before, pltpu.roll(before, 1, axis=1))
                    balance = after - before + 4.0 * wu
                    if v == 4:
                        balance = balance + decay_ref[rows, :] * (q * q * inv)
                    across_ref[v, rows, :] = balance
                    ahead_ref[v, pl.ds(8 * t + 8, 8), :] = fy[v] - wu
                    behind_ref[v, pl.ds(8 * t + 8, 8), :] = fy[v] + wu
            last = segment == len(SEGMENT_WEIGHTS) - 1
            for t in (1, 2) if last else range(4):
                rows = pl.ds(8 * t, 8)
                step = weight * step_ref[n, rows, :]
                for v in range(5):
                    total = (
                        across_ref[v, rows, :]
                        + ahead_ref[v, pl.ds(8 * t + 9, 8), :]
                        - behind_ref[v, pl.ds(8 * t + 7, 8), :]
                        + source_ref[n, v, rows, :]
                    )
                    change = step * total
                    begin = start_ref[n, v, rows, :]
                    if last:
                        out_ref[n, v, pl.ds(8 * t - 8, 8), :] = -change
                        continue
                    after = begin - change
                    if t == 0:
                        after = jnp.where(is_first, begin, after)
                    if t == 3:
                        after = jnp.where(is_last, begin, after)
                    now_ref[n, v, rows, :] = after


def local(state, wall_distance, blade_counts):
    f32 = jnp.float32
    field = functools.partial(jax.ShapeDtypeStruct, dtype=f32)
    other = lax.ppermute(state, "zh", [(0, 1), (1, 0)])
    peak, counts, state = pl.pallas_call(
        peak_kernel, out_shape=(field((8, 1, 128)), field((2,)), field(state.shape)),
        in_specs=[SMEM, VMEM], out_specs=(VMEM, SMEM, VMEM),
        compiler_params=PARAMS, name="peak",
    )(blade_counts, state)
    peaks = lax.all_to_all(peak, "y", 0, 0)
    peak = pl.pallas_call(
        fold_kernel, out_shape=field((32, 1, 128)), in_specs=[VMEM], out_specs=VMEM,
        compiler_params=PARAMS, name="fold",
    )(peaks)
    peaks = lax.all_to_all(peak, ("zl", "zh", "core"), 0, 0)
    outer = pl.pallas_call(
        partial_kernel, out_shape=field((4, 96, 512)),
        in_specs=[SMEM, VMEM, VMEM, VMEM], out_specs=VMEM,
        scratch_shapes=[pltpu.VMEM((NT, 128), f32)],
        compiler_params=PARAMS, name="partial_sources",
    )(counts, state, other, peaks)
    outer = lax.all_to_all(outer, "x", 0, 0)
    far, near, inner = pl.pallas_call(
        edge_kernel, out_shape=(field((96, 512)), field((96, 512)), field((4, 80, 512))),
        in_specs=[SMEM] + [VMEM] * 4, out_specs=(VMEM, VMEM, VMEM),
        compiler_params=PARAMS, name="edges",
    )(counts, state, other, wall_distance, outer)
    count = lax.axis_size(CELLS)
    across = [((i + 1) % count, (i + 2) % count) for i in range(0, count, 2)]
    far = lax.ppermute(far, CELLS, across + [(j, i) for i, j in across])
    near = lax.ppermute(near, "core", [(0, 1), (1, 0)])
    inner = lax.all_to_all(inner, "x", 0, 0)
    return pl.pallas_call(
        march_kernel, out_shape=field(state.shape),
        in_specs=[SMEM] + [VMEM] * 6, out_specs=VMEM,
        scratch_shapes=[
            pltpu.VMEM((2, 5, 32, 512), f32),
            pltpu.VMEM((2, 5, 32, 512), f32),
            pltpu.VMEM((2, 5, 32, 512), f32),
            pltpu.VMEM((2, 32, 512), f32),
            pltpu.VMEM((32, 512), f32),
            pltpu.VMEM((5, 32, 512), f32),
            pltpu.VMEM((5, 48, 512), f32),
            pltpu.VMEM((5, 48, 512), f32),
        ],
        compiler_params=PARAMS, name="march",
    )(counts, state, wall_distance, outer, inner, far, near)


def solution(mesh):
    fine = Mesh(mesh.devices.reshape(8, 8, 2, 4, 2), ("y", "zl", "core", "x", "zh"))
    inst = ("x", "zh")
    placed = (P(inst, None, CELLS, None), P(CELLS, None), P())
    return jax.shard_map(
        local, mesh=fine, in_specs=placed, out_specs=P(inst, None, CELLS, None), check_vma=False
    )
```

```python
import functools
import math

import jax
import jax.numpy as jnp
from jax import lax
from jax.experimental import pallas as pl
from jax.experimental.pallas import tpu as pltpu
from jax.sharding import Mesh
from jax.sharding import PartitionSpec as P

NT = 16
HALF = NT // 2
ROTATION = 0.001
SEGMENT_WEIGHTS = (0.25, 1.0 / 6.0, 0.375, 0.5, 1.0)
CELLS = ("y", "zl", "core")
VMEM = pl.BlockSpec(memory_space=pltpu.VMEM)
SMEM = pl.BlockSpec(memory_space=pltpu.SMEM)
PARAMS = pltpu.CompilerParams(vmem_limit_bytes=12 * 1024 * 1024)

SLOPE = [
    -(2.0 / NT) * sum(k * math.sin(2.0 * math.pi * k * j / NT) for k in range(1, HALF))
    for j in range(NT)
]


def omega_of(counts_ref):
    return (2.0 * math.pi * ROTATION) * counts_ref[1]


def speed_sum_and_max(r, mx, my, e):
    inv = 1.0 / r
    vx = mx * inv
    vy = my * inv
    p = 0.4 * (e - 0.5 * (mx * vx + my * vy))
    c = jnp.sqrt(1.4 * p * inv)
    ax = jnp.abs(vx)
    ay = jnp.abs(vy)
    return ax + ay + 2.0 * c, jnp.maximum(ax, ay) + c


def peak_kernel(whole_ref, state_ref, out_ref, counts_ref, held_ref):
    held_ref[...] = state_ref[...]
    for k in range(2):
        counts_ref[k] = whole_ref[k].astype(jnp.float32)
    best = None
    for n in range(2):
        for t in range(2):
            rows = pl.ds(8 * t, 8)
            _, top = speed_sum_and_max(*(state_ref[n, v, rows, :] for v in range(4)))
            best = top if best is None else jnp.maximum(best, top)
    peak = jnp.max(best, axis=(0, 1), keepdims=True)
    out_ref[...] = jnp.broadcast_to(peak[None], out_ref.shape)


def partial_kernel(counts_ref, state_ref, other_ref, peaks_ref, out_ref, lag_ref):
    me_x = lax.axis_index("x")
    peak = jnp.max(peaks_ref[...], axis=0)
    upper_half = lax.axis_index("zh")
    place = lax.axis_index(CELLS)
    is_last = place == lax.axis_size(CELLS) - 1
    omega = omega_of(counts_ref)
    ratio = jnp.full((NT, 128), counts_ref[1]) / jnp.full((NT, 128), counts_ref[0])
    sigma = 2.0 * math.pi * ratio
    shift = jnp.where(is_last, sigma, -sigma)
    offset = lax.broadcasted_iota(jnp.int32, (NT, 128), 0).astype(jnp.float32)
    order = lax.broadcasted_iota(jnp.int32, (NT, 128), 1)
    angle = (2.0 * math.pi / NT) * offset + shift
    share = jnp.where(order > HALF, 0.0, jnp.where((order == 0) | (order == HALF), 1.0, 2.0))
    terms = share * jnp.cos(order.astype(jnp.float32) * angle)
    lag_ref[...] = jnp.broadcast_to(
        jnp.sum(terms, axis=1, keepdims=True) * (1.0 / NT), lag_ref.shape
    )
    for step in range(4):
        target = lax.rem(me_x + step, 4)
        own = [[(4 * step + n - m) % NT for m in range(2)] for n in range(2)]
        high = [[(4 * step + 2 + n - m) % NT for m in range(2)] for n in range(2)]
        low = [[(4 * step - 2 + n - m) % NT for m in range(2)] for n in range(2)]
        scale = [
            [omega * SLOPE[own[n][m]] for m in range(2)]
            + [
                omega * jnp.where(upper_half == 1, SLOPE[high[n][m]], SLOPE[low[n][m]])
                for m in range(2)
            ]
            for n in range(2)
        ]
        for v in range(5):
            for t in range(2):
                rows = pl.ds(8 * t, 8)
                fields = [state_ref[m, v, rows, :] for m in range(2)] + [
                    other_ref[m, v, rows, :] for m in range(2)
                ]
                for n in range(2):
                    total = scale[n][0] * fields[0]
                    for m in range(1, 4):
                        total = total + scale[n][m] * fields[m]
                    out_ref[target, pl.ds((n * 5 + v) * 16 + 8 * t, 8), :] = total

        def lag(j):
            return jnp.concatenate([lag_ref[j : j + 1, :]] * 4, axis=1)

        factor = [
            [lag(own[n][m]) for m in range(2)]
            + [jnp.where(upper_half == 1, lag(high[n][m]), lag(low[n][m])) for m in range(2)]
            for n in range(2)
        ]
        for v in range(5):
            edges = [
                jnp.where(is_last, ref[m, v, 15:16, :], ref[m, v, 0:1, :])
                for ref in (state_ref, other_ref)
                for m in range(2)
            ]
            for n in range(2):
                total = factor[n][0] * edges[0]
                for m in range(1, 4):
                    total = total + factor[n][m] * edges[m]
                out_ref[target, pl.ds(160 + n * 5 + v, 1), :] = total
        out_ref[target, pl.ds(170, 6), :] = jnp.broadcast_to(
            jnp.concatenate([peak] * 4, axis=1), (6, 512)
        )


def edge_kernel(state_ref, wall_ref, parts_ref, far_ref, near_ref, peak_ref):
    place = lax.axis_index(CELLS)
    is_first = place == 0
    is_last = place == lax.axis_size(CELLS) - 1
    is_even = lax.axis_index("core") == 0
    row = lax.broadcasted_iota(jnp.int32, (8, 512), 0)

    def put(rows, up, down):
        far_ref[rows, :] = jnp.where(is_even, down, up)
        near_ref[rows, :] = jnp.where(is_even, up, down)

    def added(start, count):
        rows = pl.ds(start, count)
        return (parts_ref[0, rows, :] + parts_ref[1, rows, :]) + (
            parts_ref[2, rows, :] + parts_ref[3, rows, :]
        )

    for n in range(2):
        for v in range(5):
            at = n * 5 + v
            lagged = jnp.broadcast_to(added(160 + at, 1), (8, 512))
            source = pltpu.roll(added(at * 16 + 8, 8), 4, axis=0)
            up = jnp.where(row >= 4, state_ref[n, v, 8:16, :], source)
            up = jnp.where(is_last & (row == 7), lagged, up)
            source = pltpu.roll(added(at * 16, 8), 4, axis=0)
            down = jnp.where(row < 4, state_ref[n, v, 0:8, :], source)
            down = jnp.where(is_first & (row == 0), lagged, down)
            put(pl.ds(at * 8, 8), up, down)
            put(pl.ds(80 + at, 1), state_ref[n, v, 11:12, :], state_ref[n, v, 4:5, :])
    put(pl.ds(90, 4), wall_ref[12:16, :], wall_ref[0:4, :])
    put(pl.ds(94, 2), wall_ref[14:16, :], wall_ref[0:2, :])
    peak = parts_ref[0, 170:171, 0:128]
    for k in range(1, 4):
        peak = jnp.maximum(peak, parts_ref[k, 170:171, 0:128])
    peak_ref[...] = jnp.broadcast_to(peak[None], peak_ref.shape)


def march_kernel(
    counts_ref,
    state_ref,
    wall_ref,
    parts_ref,
    far_ref,
    near_ref,
    peaks_ref,
    out_ref,
    start_ref,
    now_ref,
    source_ref,
    step_ref,
    decay_ref,
    across_ref,
    ahead_ref,
    behind_ref,
):
    place = lax.axis_index(CELLS)
    is_first = place == 0
    is_last = place == lax.axis_size(CELLS) - 1
    omega = omega_of(counts_ref)
    row = lax.broadcasted_iota(jnp.int32, (8, 512), 0)
    column = lax.broadcasted_iota(jnp.int32, (8, 512), 1)
    at_left = column == 0
    at_right = column == 511
    is_even = lax.axis_index("core") == 0

    def lower(rows):
        return jnp.where(is_even, far_ref[rows, :], near_ref[rows, :])

    def upper(rows):
        return jnp.where(is_even, near_ref[rows, :], far_ref[rows, :])

    peak = jnp.max(peaks_ref[...], axis=0)
    peak = jnp.concatenate([peak] * 4, axis=1)
    wave = jnp.broadcast_to(peak, (8, 512))

    walls = [
        jnp.concatenate([lower(pl.ds(90, 4))] * 2, axis=0),
        wall_ref[0:8, :],
        wall_ref[8:16, :],
        jnp.concatenate([upper(pl.ds(90, 4))] * 2, axis=0),
    ]
    for t in range(4):
        decay_ref[pl.ds(8 * t, 8), :] = 0.8 / (walls[t] * walls[t])
    for n in range(2):
        for v in range(5):
            at = n * 5 + v
            packed = lower(pl.ds(at * 8, 8))
            fifth = jnp.broadcast_to(lower(pl.ds(80 + at, 1)), (8, 512))
            start_ref[n, v, 0:8, :] = jnp.where(row >= 4, packed, fifth)
            source_ref[n, v, 0:8, :] = 2.0 * pltpu.roll(packed, 4, axis=0)
            packed = upper(pl.ds(at * 8, 8))
            fifth = jnp.broadcast_to(upper(pl.ds(80 + at, 1)), (8, 512))
            start_ref[n, v, 24:32, :] = jnp.where(row < 4, packed, fifth)
            source_ref[n, v, 24:32, :] = 2.0 * pltpu.roll(packed, 4, axis=0)
            start_ref[n, v, 8:24, :] = state_ref[n, v, :, :]
            rows = pl.ds(at * 16, 16)
            total = (parts_ref[0, rows, :] + parts_ref[1, rows, :]) + (
                parts_ref[2, rows, :] + parts_ref[3, rows, :]
            )
            source_ref[n, v, 8:24, :] = 2.0 * total
        for t in range(4):
            rows = pl.ds(8 * t, 8)
            both, _ = speed_sum_and_max(*(start_ref[n, v, rows, :] for v in range(4)))
            step_ref[n, rows, :] = 0.5 / (both + omega * HALF)

    for segment, weight in enumerate(SEGMENT_WEIGHTS):
        from_ref = start_ref if segment == 0 else now_ref
        for n in range(2):
            for t in range(4):
                rows = pl.ds(8 * t, 8)
                r, mx, my, e, q = (from_ref[n, v, rows, :] for v in range(5))
                inv = 1.0 / r
                vx = mx * inv
                vy = my * inv
                p = 0.4 * (e - 0.5 * (mx * vx + my * vy))
                h = e + p
                fx = (mx, mx * vx + p, my * vx, h * vx, q * vx)
                fy = (my, mx * vy, my * vy + p, h * vy, q * vy)
                for v, u in enumerate((r, mx, my, e, q)):
                    wu = wave * u
                    after = fx[v] - wu
                    before = fx[v] + wu
                    after = jnp.where(at_right, after, pltpu.roll(after, 511, axis=1))
                    before = jnp.where(at_left, before, pltpu.roll(before, 1, axis=1))
                    balance = after - before + 4.0 * wu
                    if v == 4:
                        balance = balance + decay_ref[rows, :] * (q * q * inv)
                    across_ref[v, rows, :] = balance
                    ahead_ref[v, pl.ds(8 * t + 8, 8), :] = fy[v] - wu
                    behind_ref[v, pl.ds(8 * t + 8, 8), :] = fy[v] + wu
            last = segment == len(SEGMENT_WEIGHTS) - 1
            for t in (1, 2) if last else range(4):
                rows = pl.ds(8 * t, 8)
                step = weight * step_ref[n, rows, :]
                for v in range(5):
                    total = (
                        across_ref[v, rows, :]
                        + ahead_ref[v, pl.ds(8 * t + 9, 8), :]
                        - behind_ref[v, pl.ds(8 * t + 7, 8), :]
                        + source_ref[n, v, rows, :]
                    )
                    change = step * total
                    begin = start_ref[n, v, rows, :]
                    if last:
                        out_ref[n, v, pl.ds(8 * t - 8, 8), :] = -change
                        continue
                    after = begin - change
                    if t == 0:
                        after = jnp.where(is_first, begin, after)
                    if t == 3:
                        after = jnp.where(is_last, begin, after)
                    now_ref[n, v, rows, :] = after


def local(state, wall_distance, blade_counts):
    f32 = jnp.float32
    field = functools.partial(jax.ShapeDtypeStruct, dtype=f32)
    other = lax.ppermute(state, "zh", [(0, 1), (1, 0)])
    peak, counts, state = pl.pallas_call(
        peak_kernel, out_shape=(field((8, 1, 128)), field((2,)), field(state.shape)),
        in_specs=[SMEM, VMEM], out_specs=(VMEM, SMEM, VMEM),
        compiler_params=PARAMS, name="peak",
    )(blade_counts, state)
    peaks = lax.all_to_all(peak, "y", 0, 0)
    parts = pl.pallas_call(
        partial_kernel, out_shape=field((4, 176, 512)),
        in_specs=[SMEM, VMEM, VMEM, VMEM], out_specs=VMEM,
        scratch_shapes=[pltpu.VMEM((NT, 128), f32)],
        compiler_params=PARAMS, name="partial_sources",
    )(counts, state, other, peaks)
    parts = lax.all_to_all(parts, "x", 0, 0)
    far, near, peak = pl.pallas_call(
        edge_kernel, out_shape=(field((96, 512)), field((96, 512)), field((32, 1, 128))),
        in_specs=[VMEM] * 3, out_specs=(VMEM, VMEM, VMEM),
        compiler_params=PARAMS, name="edges",
    )(state, wall_distance, parts)
    count = lax.axis_size(CELLS)
    across = [((i + 1) % count, (i + 2) % count) for i in range(0, count, 2)]
    far = lax.ppermute(far, CELLS, across + [(j, i) for i, j in across])
    near = lax.ppermute(near, "core", [(0, 1), (1, 0)])
    peaks = lax.all_to_all(peak, ("zl", "zh", "core"), 0, 0)
    return pl.pallas_call(
        march_kernel, out_shape=field(state.shape),
        in_specs=[SMEM] + [VMEM] * 6, out_specs=VMEM,
        scratch_shapes=[
            pltpu.VMEM((2, 5, 32, 512), f32),
            pltpu.VMEM((2, 5, 32, 512), f32),
            pltpu.VMEM((2, 5, 32, 512), f32),
            pltpu.VMEM((2, 32, 512), f32),
            pltpu.VMEM((32, 512), f32),
            pltpu.VMEM((5, 32, 512), f32),
            pltpu.VMEM((5, 48, 512), f32),
            pltpu.VMEM((5, 48, 512), f32),
        ],
        compiler_params=PARAMS, name="march",
    )(counts, state, wall_distance, parts, far, near, peaks)


def solution(mesh):
    fine = Mesh(mesh.devices.reshape(8, 8, 2, 4, 2), ("y", "zl", "core", "x", "zh"))
    inst = ("x", "zh")
    placed = (P(inst, None, CELLS, None), P(CELLS, None), P())
    return jax.shard_map(
        local, mesh=fine, in_specs=placed, out_specs=P(inst, None, CELLS, None), check_vma=False
    )
```

```python
import math

import jax
import jax.numpy as jnp
from jax import lax
from jax.experimental import pallas as pl
from jax.experimental.pallas import tpu as pltpu
from jax.sharding import Mesh
from jax.sharding import PartitionSpec as P

NT = 16
HALF = NT // 2
ROTATION = 0.001
SEGMENT_WEIGHTS = (0.25, 1.0 / 6.0, 0.375, 0.5, 1.0)
CELLS = ("y", "zl", "core")
VMEM = pl.BlockSpec(memory_space=pltpu.VMEM)
SMEM = pl.BlockSpec(memory_space=pltpu.SMEM)
PARAMS = pltpu.CompilerParams(vmem_limit_bytes=12 * 1024 * 1024)

SLOPE = [
    -(2.0 / NT) * sum(k * math.sin(2.0 * math.pi * k * j / NT) for k in range(1, HALF))
    for j in range(NT)
]


def omega_of(counts_ref):
    return (2.0 * math.pi * ROTATION) * counts_ref[1]


def speed_sum_and_max(r, mx, my, e):
    inv = 1.0 / r
    vx = mx * inv
    vy = my * inv
    p = 0.4 * (e - 0.5 * (mx * vx + my * vy))
    c = jnp.sqrt(1.4 * p * inv)
    ax = jnp.abs(vx)
    ay = jnp.abs(vy)
    return ax + ay + 2.0 * c, jnp.maximum(ax, ay) + c


def prepare_kernel(whole_ref, state_ref, outer_ref, inner_ref, blocks_ref, counts_ref):
    for k in range(2):
        counts_ref[k] = whole_ref[k].astype(jnp.float32)
    row = lax.broadcasted_iota(jnp.int32, (8, 512), 0)
    for n in range(2):
        for v in range(5):
            first = state_ref[n, v, 0:8, :]
            second = state_ref[n, v, 8:16, :]
            rows = pl.ds((n * 5 + v) * 8, 8)
            outer = jnp.where(row < 4, first, second)
            outer_ref[rows, :] = outer
            inner_ref[rows, :] = jnp.where(row < 4, second, first)
            for k in range(4):
                blocks_ref[k, rows, :] = outer[:, 128 * k : 128 * k + 128]


def peak_kernel(mine_ref, inside_ref, _, peak_ref):
    best = None
    for ref in (mine_ref, inside_ref):
        for n in range(2):
            _, top = speed_sum_and_max(*(ref[pl.ds((n * 5 + v) * 8, 8), :] for v in range(4)))
            best = top if best is None else jnp.maximum(best, top)
    peak = jnp.max(best, axis=(0, 1), keepdims=True)
    peak_ref[...] = jnp.broadcast_to(peak[None], peak_ref.shape)


def fold_kernel(peaks_ref, out_ref):
    peak = jnp.max(peaks_ref[...], axis=0)
    out_ref[...] = jnp.broadcast_to(peak[None], out_ref.shape)


def add_partials(counts_ref, mine_ref, other_ref, out_ref):
    me_x = lax.axis_index("x")
    upper_half = lax.axis_index("zh")
    omega = omega_of(counts_ref)
    for v in range(5):
        fields = [
            ref[pl.ds((m * 5 + v) * 8, 8), :] for ref in (mine_ref, other_ref) for m in range(2)
        ]
        for step in range(4):
            target = lax.rem(me_x + step, 4)
            for n in range(2):
                total = None
                for m, field in enumerate(fields):
                    own, high, low = offsets(step, n, m)
                    factor = SLOPE[own]
                    if m >= 2:
                        factor = jnp.where(upper_half == 1, SLOPE[high], SLOPE[low])
                    term = (omega * factor) * field
                    total = term if total is None else total + term
                out_ref[target, pl.ds((n * 5 + v) * 8, 8), :] = total


def offsets(step, n, m):
    apart = 4 * step + n - m % 2
    return apart % NT, (apart + 2) % NT, (apart - 2) % NT


def outer_kernel(counts_ref, ours_ref, theirs_ref, peaks_ref, _, out_ref, lag_ref):
    upper_half = lax.axis_index("zh")
    place = lax.axis_index(CELLS)
    is_last = place == lax.axis_size(CELLS) - 1
    omega = omega_of(counts_ref)
    ratio = jnp.full((NT, 128), counts_ref[1]) / jnp.full((NT, 128), counts_ref[0])
    sigma = 2.0 * math.pi * ratio
    shift = jnp.where(is_last, sigma, -sigma)
    offset = lax.broadcasted_iota(jnp.int32, (NT, 128), 0).astype(jnp.float32)
    order = lax.broadcasted_iota(jnp.int32, (NT, 128), 1)
    angle = (2.0 * math.pi / NT) * offset + shift
    share = jnp.where(order > HALF, 0.0, jnp.where((order == 0) | (order == HALF), 1.0, 2.0))
    terms = share * jnp.cos(order.astype(jnp.float32) * angle)
    lag_ref[...] = jnp.broadcast_to(
        jnp.sum(terms, axis=1, keepdims=True) * (1.0 / NT), lag_ref.shape
    )
    slopes, lags = [], []
    for j in range(NT):
        high, low = (j + 2) % NT, (j - 2) % NT
        across = jnp.where(upper_half == 1, SLOPE[high], SLOPE[low])
        slopes.append((omega * SLOPE[j], omega * across))
        high, low = lag_ref[high : high + 1, :], lag_ref[low : low + 1, :]
        lags.append((lag_ref[j : j + 1, :], jnp.where(upper_half == 1, high, low)))
    peak = jnp.broadcast_to(jnp.max(peaks_ref[...], axis=0), (6, 128))
    for v in range(5):
        sums = [None] * 8
        rims = [None] * 8
        for half, ref in enumerate((ours_ref, theirs_ref)):
            for m in range(8):
                at = ((m % 2) * 5 + v) * 8
                field = ref[m // 2, pl.ds(at, 8), :]
                rim = jnp.where(is_last, field[7:8, :], field[0:1, :])
                for n in range(8):
                    apart = (4 * (n // 2 - m // 2) + n % 2 - m % 2) % NT
                    term = slopes[apart][half] * field
                    sums[n] = term if sums[n] is None else sums[n] + term
                    term = lags[apart][half] * rim
                    rims[n] = term if rims[n] is None else rims[n] + term
        for n in range(8):
            at = (n % 2) * 5 + v
            out_ref[n // 2, pl.ds(at * 8, 8), :] = sums[n]
            out_ref[n // 2, pl.ds(80 + at, 1), :] = rims[n]
    for k in range(4):
        out_ref[k, pl.ds(90, 6), :] = peak


def joined(blocks_ref, start, count):
    return jnp.concatenate([blocks_ref[k, pl.ds(start, count), :] for k in range(4)], axis=1)


def added(parts_ref, start, count):
    rows = pl.ds(start, count)
    return (parts_ref[0, rows, :] + parts_ref[1, rows, :]) + (
        parts_ref[2, rows, :] + parts_ref[3, rows, :]
    )


def edge_kernel(
    counts_ref, mine_ref, inside_ref, other_ref, wall_ref, outer_ref,
    far_ref, near_ref, inner_ref,
):
    add_partials(counts_ref, inside_ref, other_ref, inner_ref)
    place = lax.axis_index(CELLS)
    is_first = place == 0
    is_last = place == lax.axis_size(CELLS) - 1
    is_even = lax.axis_index("core") == 0
    row = lax.broadcasted_iota(jnp.int32, (8, 512), 0)

    def put(rows, up, down):
        far_ref[rows, :] = jnp.where(is_even, down, up)
        near_ref[rows, :] = jnp.where(is_even, up, down)

    for n in range(2):
        for v in range(5):
            at = n * 5 + v
            lagged = jnp.broadcast_to(joined(outer_ref, 80 + at, 1), (8, 512))
            source = pltpu.roll(joined(outer_ref, at * 8, 8), 4, axis=0)
            mine = mine_ref[pl.ds(at * 8, 8), :]
            up = jnp.where(row >= 4, mine, source)
            up = jnp.where(is_last & (row == 7), lagged, up)
            down = jnp.where(row < 4, mine, source)
            down = jnp.where(is_first & (row == 0), lagged, down)
            put(pl.ds(at * 8, 8), up, down)
            put(
                pl.ds(80 + at, 1),
                inside_ref[pl.ds(at * 8 + 3, 1), :],
                inside_ref[pl.ds(at * 8 + 4, 1), :],
            )
    put(pl.ds(90, 4), wall_ref[12:16, :], wall_ref[0:4, :])
    put(pl.ds(94, 2), wall_ref[14:16, :], wall_ref[0:2, :])


def march_kernel(
    counts_ref,
    mine_ref,
    inside_ref,
    wall_ref,
    outer_ref,
    inner_ref,
    far_ref,
    near_ref,
    out_ref,
    start_ref,
    now_ref,
    source_ref,
    step_ref,
    decay_ref,
    across_ref,
    ahead_ref,
    behind_ref,
):
    place = lax.axis_index(CELLS)
    is_first = place == 0
    is_last = place == lax.axis_size(CELLS) - 1
    omega = omega_of(counts_ref)
    row = lax.broadcasted_iota(jnp.int32, (8, 512), 0)
    column = lax.broadcasted_iota(jnp.int32, (8, 512), 1)
    at_left = column == 0
    at_right = column == 511
    is_even = lax.axis_index("core") == 0

    def lower(rows):
        return jnp.where(is_even, far_ref[rows, :], near_ref[rows, :])

    def upper(rows):
        return jnp.where(is_even, near_ref[rows, :], far_ref[rows, :])

    peak = outer_ref[0, 90:91, :]
    for k in range(1, 4):
        peak = jnp.maximum(peak, outer_ref[k, 90:91, :])
    peak = jnp.concatenate([peak] * 4, axis=1)
    wave = jnp.broadcast_to(peak, (8, 512))

    walls = [
        jnp.concatenate([lower(pl.ds(90, 4))] * 2, axis=0),
        wall_ref[0:8, :],
        wall_ref[8:16, :],
        jnp.concatenate([upper(pl.ds(90, 4))] * 2, axis=0),
    ]
    for t in range(4):
        decay_ref[pl.ds(8 * t, 8), :] = 0.8 / (walls[t] * walls[t])
    for n in range(2):
        for v in range(5):
            at = n * 5 + v
            packed = lower(pl.ds(at * 8, 8))
            fifth = jnp.broadcast_to(lower(pl.ds(80 + at, 1)), (8, 512))
            start_ref[n, v, 0:8, :] = jnp.where(row >= 4, packed, fifth)
            source_ref[n, v, 0:8, :] = 2.0 * pltpu.roll(packed, 4, axis=0)
            packed = upper(pl.ds(at * 8, 8))
            fifth = jnp.broadcast_to(upper(pl.ds(80 + at, 1)), (8, 512))
            start_ref[n, v, 24:32, :] = jnp.where(row < 4, packed, fifth)
            source_ref[n, v, 24:32, :] = 2.0 * pltpu.roll(packed, 4, axis=0)
            mine = mine_ref[pl.ds(at * 8, 8), :]
            inside = inside_ref[pl.ds(at * 8, 8), :]
            start_ref[n, v, 8:16, :] = jnp.where(row < 4, mine, inside)
            start_ref[n, v, 16:24, :] = jnp.where(row < 4, inside, mine)
            outer = 2.0 * joined(outer_ref, at * 8, 8)
            inner = 2.0 * added(inner_ref, at * 8, 8)
            source_ref[n, v, 8:16, :] = jnp.where(row < 4, outer, inner)
            source_ref[n, v, 16:24, :] = jnp.where(row < 4, inner, outer)
        for t in range(4):
            rows = pl.ds(8 * t, 8)
            both, _ = speed_sum_and_max(*(start_ref[n, v, rows, :] for v in range(4)))
            step_ref[n, rows, :] = 0.5 / (both + omega * HALF)

    for segment, weight in enumerate(SEGMENT_WEIGHTS):
        from_ref = start_ref if segment == 0 else now_ref
        for n in range(2):
            for t in range(4):
                rows = pl.ds(8 * t, 8)
                r, mx, my, e, q = (from_ref[n, v, rows, :] for v in range(5))
                inv = 1.0 / r
                vx = mx * inv
                vy = my * inv
                p = 0.4 * (e - 0.5 * (mx * vx + my * vy))
                h = e + p
                fx = (mx, mx * vx + p, my * vx, h * vx, q * vx)
                fy = (my, mx * vy, my * vy + p, h * vy, q * vy)
                for v, u in enumerate((r, mx, my, e, q)):
                    wu = wave * u
                    after = fx[v] - wu
                    before = fx[v] + wu
                    after = jnp.where(at_right, after, pltpu.roll(after, 511, axis=1))
                    before = jnp.where(at_left, before, pltpu.roll(before, 1, axis=1))
                    balance = after - before + 4.0 * wu
                    if v == 4:
                        balance = balance + decay_ref[rows, :] * (q * q * inv)
                    across_ref[v, rows, :] = balance
                    ahead_ref[v, pl.ds(8 * t + 8, 8), :] = fy[v] - wu
                    behind_ref[v, pl.ds(8 * t + 8, 8), :] = fy[v] + wu
            last = segment == len(SEGMENT_WEIGHTS) - 1
            for t in (1, 2) if last else range(4):
                rows = pl.ds(8 * t, 8)
                step = weight * step_ref[n, rows, :]
                for v in range(5):
                    total = (
                        across_ref[v, rows, :]
                        + ahead_ref[v, pl.ds(8 * t + 9, 8), :]
                        - behind_ref[v, pl.ds(8 * t + 7, 8), :]
                        + source_ref[n, v, rows, :]
                    )
                    change = step * total
                    begin = start_ref[n, v, rows, :]
                    if last:
                        out_ref[n, v, pl.ds(8 * t - 8, 8), :] = -change
                        continue
                    after = begin - change
                    if t == 0:
                        after = jnp.where(is_first, begin, after)
                    if t == 3:
                        after = jnp.where(is_last, begin, after)
                    now_ref[n, v, rows, :] = after


def call(kernel, name, shapes, spaces, *operands, scratch=()):
    f32 = jnp.float32
    out_shape = [jax.ShapeDtypeStruct(shape, f32) for shape in shapes]
    return pl.pallas_call(
        kernel, out_shape=out_shape, name=name, compiler_params=PARAMS,
        in_specs=[SMEM if x.shape == (2,) else VMEM for x in operands], out_specs=spaces,
        scratch_shapes=[pltpu.VMEM(shape, f32) for shape in scratch],
    )(*operands)


def local(state, wall_distance, blade_counts):
    swap = [(0, 1), (1, 0)]
    half = (80, 512)
    mine, inside, blocks, counts = call(
        prepare_kernel, "prepare", [half, half, (4, 80, 128), (2,)], [VMEM] * 3 + [SMEM],
        blade_counts, state,
    )
    other_inside = lax.ppermute(inside, "zh", swap)
    ours = lax.all_to_all(blocks, "x", 0, 0)
    theirs = lax.ppermute(ours, "zh", swap)
    (peak,) = call(peak_kernel, "peak", [(8, 1, 128)], [VMEM], mine, inside, ours)
    peaks = lax.all_to_all(peak, "y", 0, 0)
    (peak,) = call(fold_kernel, "fold", [(32, 1, 128)], [VMEM], peaks)
    peaks = lax.all_to_all(peak, ("zl", "zh", "core"), 0, 0)
    (outer,) = call(
        outer_kernel, "outer_sources", [(4, 96, 128)], [VMEM],
        counts, ours, theirs, peaks, other_inside, scratch=[(NT, 128)],
    )
    outer = lax.all_to_all(outer, "x", 0, 0)
    far, near, inner = call(
        edge_kernel, "edges", [(96, 512), (96, 512), (4, 80, 512)], [VMEM] * 3,
        counts, mine, inside, other_inside, wall_distance, outer,
    )
    count = lax.axis_size(CELLS)
    across = [((i + 1) % count, (i + 2) % count) for i in range(0, count, 2)]
    far = lax.ppermute(far, CELLS, across + [(j, i) for i, j in across])
    near = lax.ppermute(near, "core", swap)
    inner = lax.all_to_all(inner, "x", 0, 0)
    (change,) = call(
        march_kernel, "march", [state.shape], [VMEM],
        counts, mine, inside, wall_distance, outer, inner, far, near,
        scratch=[
            (2, 5, 32, 512), (2, 5, 32, 512), (2, 5, 32, 512), (2, 32, 512), (32, 512),
            (5, 32, 512), (5, 48, 512), (5, 48, 512),
        ],
    )
    return change


def solution(mesh):
    fine = Mesh(mesh.devices.reshape(8, 8, 2, 4, 2), ("y", "zl", "core", "x", "zh"))
    inst = ("x", "zh")
    placed = (P(inst, None, CELLS, None), P(CELLS, None), P())
    return jax.shard_map(
        local, mesh=fine, in_specs=placed, out_specs=P(inst, None, CELLS, None), check_vma=False
    )
```

```python
import functools
import math

import jax
import jax.numpy as jnp
from jax import lax
from jax.experimental import pallas as pl
from jax.experimental.pallas import tpu as pltpu
from jax.sharding import Mesh
from jax.sharding import PartitionSpec as P

NT = 16
HALF = NT // 2
ROTATION = 0.001
SEGMENT_WEIGHTS = (0.25, 1.0 / 6.0, 0.375, 0.5, 1.0)
CELLS = ("y", "zl", "core")
VMEM = pl.BlockSpec(memory_space=pltpu.VMEM)
SMEM = pl.BlockSpec(memory_space=pltpu.SMEM)
PARAMS = pltpu.CompilerParams(vmem_limit_bytes=12 * 1024 * 1024)

SLOPE = [
    -(2.0 / NT) * sum(k * math.sin(2.0 * math.pi * k * j / NT) for k in range(1, HALF))
    for j in range(NT)
]


def omega_of(counts_ref):
    return (2.0 * math.pi * ROTATION) * counts_ref[1]


def speed_sum_and_max(r, mx, my, e):
    inv = 1.0 / r
    vx = mx * inv
    vy = my * inv
    p = 0.4 * (e - 0.5 * (mx * vx + my * vy))
    c = jnp.sqrt(1.4 * p * inv)
    ax = jnp.abs(vx)
    ay = jnp.abs(vy)
    return ax + ay + 2.0 * c, jnp.maximum(ax, ay) + c


def peak_kernel(whole_ref, state_ref, out_ref, counts_ref, held_ref):
    held_ref[...] = state_ref[...]
    for k in range(2):
        counts_ref[k] = whole_ref[k].astype(jnp.float32)
    best = None
    for n in range(2):
        for t in range(2):
            rows = pl.ds(8 * t, 8)
            _, top = speed_sum_and_max(*(state_ref[n, v, rows, :] for v in range(4)))
            best = top if best is None else jnp.maximum(best, top)
    peak = jnp.max(best, axis=(0, 1), keepdims=True)
    out_ref[...] = jnp.broadcast_to(peak[None], out_ref.shape)


def fold_kernel(peaks_ref, out_ref):
    peak = jnp.max(peaks_ref[...], axis=0)
    out_ref[...] = jnp.broadcast_to(peak[None], out_ref.shape)


def combine(counts_ref, fields, crossing, step, n):
    omega = omega_of(counts_ref)
    total = None
    for m, field in enumerate(fields):
        own, high, low = offsets(step, n, m)
        factor = SLOPE[own]
        if m >= 2:
            factor = jnp.where(crossing, SLOPE[high], SLOPE[low])
        term = (omega * factor) * field
        total = term if total is None else total + term
    return total


def add_partials(counts_ref, state_ref, other_ref, out_ref, edge):
    me_x = lax.axis_index("x")
    is_upper = lax.axis_index("zh") == 1
    is_even = lax.axis_index("core") == 0
    row = lax.broadcasted_iota(jnp.int32, (8, 512), 0)
    for v in range(5):
        fields = [
            jnp.where((row < 4) == edge, ref[m, v, 0:8, :], ref[m, v, 8:16, :])
            for ref in (state_ref, other_ref)
            for m in range(2)
        ]
        if edge:
            turned = [jnp.where(is_even, f, pltpu.roll(f, 4, axis=0)) for f in fields]
            turned = turned[2:] + turned[:2]
        for step in range(4):
            target = lax.rem(me_x + step, 4)
            for n in range(2):
                total = combine(counts_ref, fields, is_upper, step, n)
                out_ref[target, pl.ds((n * 5 + v) * 8, 8), :] = total
            if edge:
                first, second = (
                    combine(counts_ref, turned, jnp.logical_not(is_upper), step, n)
                    for n in range(2)
                )
                out_ref[target, pl.ds(96 + v * 8, 8), :] = jnp.where(
                    row < 4, first, pltpu.roll(second, 4, axis=0)
                )


def offsets(step, n, m):
    apart = 4 * step + n - m % 2
    return apart % NT, (apart + 2) % NT, (apart - 2) % NT


def partial_kernel(counts_ref, state_ref, other_ref, peaks_ref, out_ref, lag_ref):
    me_x = lax.axis_index("x")
    is_lower = lax.axis_index("zh") == 0
    place = lax.axis_index(CELLS)
    is_last = place == lax.axis_size(CELLS) - 1
    add_partials(counts_ref, state_ref, other_ref, out_ref, True)
    ratio = jnp.full((NT, 128), counts_ref[1]) / jnp.full((NT, 128), counts_ref[0])
    sigma = 2.0 * math.pi * ratio
    shift = jnp.where(is_last, sigma, -sigma)
    offset = lax.broadcasted_iota(jnp.int32, (NT, 128), 0).astype(jnp.float32)
    order = lax.broadcasted_iota(jnp.int32, (NT, 128), 1)
    angle = (2.0 * math.pi / NT) * offset + shift
    share = jnp.where(order > HALF, 0.0, jnp.where((order == 0) | (order == HALF), 1.0, 2.0))
    terms = share * jnp.cos(order.astype(jnp.float32) * angle)
    lag_ref[...] = jnp.broadcast_to(
        jnp.sum(terms, axis=1, keepdims=True) * (1.0 / NT), lag_ref.shape
    )

    def lag(j):
        return jnp.concatenate([lag_ref[j : j + 1, :]] * 4, axis=1)

    peak = jnp.max(peaks_ref[...], axis=0)
    peak = jnp.broadcast_to(jnp.concatenate([peak] * 4, axis=1), (6, 512))
    for step in range(4):
        target = lax.rem(me_x + step, 4)
        for n in range(2):
            factor = []
            for m in range(4):
                own, high, low = offsets(step, n, m)
                factor.append(
                    lag(own) if m < 2 else jnp.where(is_lower, lag(high), lag(low))
                )
            for v in range(5):
                total = None
                for m, ref in enumerate((other_ref, other_ref, state_ref, state_ref)):
                    edge = jnp.where(is_last, ref[m % 2, v, 15:16, :], ref[m % 2, v, 0:1, :])
                    term = factor[m] * edge
                    total = term if total is None else total + term
                out_ref[target, pl.ds(80 + n * 5 + v, 1), :] = total
        out_ref[target, pl.ds(90, 6), :] = peak


def added(parts_ref, start, count):
    rows = pl.ds(start, count)
    return (parts_ref[0, rows, :] + parts_ref[1, rows, :]) + (
        parts_ref[2, rows, :] + parts_ref[3, rows, :]
    )


def edge_kernel(counts_ref, state_ref, other_ref, wall_ref, outer_ref, far_ref, near_ref, inner_ref):
    place = lax.axis_index(CELLS)
    is_first = place == 0
    is_last = place == lax.axis_size(CELLS) - 1
    is_even = lax.axis_index("core") == 0
    row = lax.broadcasted_iota(jnp.int32, (8, 512), 0)

    def put(rows, up, down):
        far_ref[rows, :] = jnp.where(is_even, down, up)
        near_ref[rows, :] = jnp.where(is_even, up, down)

    is_low_end = is_even & (lax.axis_index("zl") == 0)
    is_high_end = jnp.logical_not(is_even) & (
        lax.axis_index("zl") == lax.axis_size("zl") - 1
    )
    is_end = is_low_end | is_high_end
    near_half = (row < 4) == is_even
    for v in range(5):
        extra = added(outer_ref, 96 + v * 8, 8)
        turned = pltpu.roll(extra, 4, axis=0)
        for n in range(2):
            at = n * 5 + v
            rows = pl.ds(at * 8, 8)
            fifth = pl.ds(80 + at, 1)
            source = pltpu.roll(added(outer_ref, at * 8, 8), 4, axis=0)
            up = jnp.where(row >= 4, state_ref[n, v, 8:16, :], source)
            down = jnp.where(row < 4, state_ref[n, v, 0:8, :], source)
            near_ref[rows, :] = jnp.where(is_even, up, down)
            near_ref[fifth, :] = jnp.where(
                is_even, state_ref[n, v, 11:12, :], state_ref[n, v, 4:5, :]
            )
            far = jnp.where(is_even, down, up)
            lagged = jnp.broadcast_to(added(outer_ref, 80 + at, 1), (8, 512))
            theirs = jnp.where(is_even, other_ref[n, v, 0:8, :], other_ref[n, v, 8:16, :])
            source = jnp.where(is_even, turned, extra) if n == 0 else jnp.where(is_even, extra, turned)
            theirs = jnp.where(near_half, theirs, source)
            theirs = jnp.where((is_first & (row == 0)) | (is_last & (row == 7)), lagged, theirs)
            far_ref[rows, :] = jnp.where(is_end, theirs, far)
            low, high = (
                jnp.where(is_end, other_ref[n, v, k : k + 1, :], state_ref[n, v, k : k + 1, :])
                for k in (4, 11)
            )
            far_ref[fifth, :] = jnp.where(is_even, low, high)
    put(pl.ds(90, 4), wall_ref[12:16, :], wall_ref[0:4, :])
    put(pl.ds(94, 2), wall_ref[14:16, :], wall_ref[0:2, :])
    add_partials(counts_ref, state_ref, other_ref, inner_ref, False)


def march_kernel(
    counts_ref,
    state_ref,
    wall_ref,
    outer_ref,
    inner_ref,
    far_ref,
    near_ref,
    out_ref,
    start_ref,
    now_ref,
    source_ref,
    step_ref,
    decay_ref,
    across_ref,
    ahead_ref,
    behind_ref,
):
    place = lax.axis_index(CELLS)
    is_first = place == 0
    is_last = place == lax.axis_size(CELLS) - 1
    omega = omega_of(counts_ref)
    row = lax.broadcasted_iota(jnp.int32, (8, 512), 0)
    column = lax.broadcasted_iota(jnp.int32, (8, 512), 1)
    at_left = column == 0
    at_right = column == 511
    is_even = lax.axis_index("core") == 0

    def lower(rows):
        return jnp.where(is_even, far_ref[rows, :], near_ref[rows, :])

    def upper(rows):
        return jnp.where(is_even, near_ref[rows, :], far_ref[rows, :])

    peak = outer_ref[0, 90:91, :]
    for k in range(1, 4):
        peak = jnp.maximum(peak, outer_ref[k, 90:91, :])
    wave = jnp.broadcast_to(peak, (8, 512))

    walls = [
        jnp.concatenate([lower(pl.ds(90, 4))] * 2, axis=0),
        wall_ref[0:8, :],
        wall_ref[8:16, :],
        jnp.concatenate([upper(pl.ds(90, 4))] * 2, axis=0),
    ]
    for t in range(4):
        decay_ref[pl.ds(8 * t, 8), :] = 0.8 / (walls[t] * walls[t])
    for n in range(2):
        for v in range(5):
            at = n * 5 + v
            packed = lower(pl.ds(at * 8, 8))
            fifth = jnp.broadcast_to(lower(pl.ds(80 + at, 1)), (8, 512))
            start_ref[n, v, 0:8, :] = jnp.where(row >= 4, packed, fifth)
            source_ref[n, v, 0:8, :] = 2.0 * pltpu.roll(packed, 4, axis=0)
            packed = upper(pl.ds(at * 8, 8))
            fifth = jnp.broadcast_to(upper(pl.ds(80 + at, 1)), (8, 512))
            start_ref[n, v, 24:32, :] = jnp.where(row < 4, packed, fifth)
            source_ref[n, v, 24:32, :] = 2.0 * pltpu.roll(packed, 4, axis=0)
            start_ref[n, v, 8:24, :] = state_ref[n, v, :, :]
            outer = 2.0 * added(outer_ref, at * 8, 8)
            inner = 2.0 * added(inner_ref, at * 8, 8)
            source_ref[n, v, 8:16, :] = jnp.where(row < 4, outer, inner)
            source_ref[n, v, 16:24, :] = jnp.where(row < 4, inner, outer)
        for t in range(4):
            rows = pl.ds(8 * t, 8)
            both, _ = speed_sum_and_max(*(start_ref[n, v, rows, :] for v in range(4)))
            step_ref[n, rows, :] = 0.5 / (both + omega * HALF)

    for segment, weight in enumerate(SEGMENT_WEIGHTS):
        from_ref = start_ref if segment == 0 else now_ref
        for n in range(2):
            for t in range(4):
                rows = pl.ds(8 * t, 8)
                r, mx, my, e, q = (from_ref[n, v, rows, :] for v in range(5))
                inv = 1.0 / r
                vx = mx * inv
                vy = my * inv
                p = 0.4 * (e - 0.5 * (mx * vx + my * vy))
                h = e + p
                fx = (mx, mx * vx + p, my * vx, h * vx, q * vx)
                fy = (my, mx * vy, my * vy + p, h * vy, q * vy)
                for v, u in enumerate((r, mx, my, e, q)):
                    wu = wave * u
                    after = fx[v] - wu
                    before = fx[v] + wu
                    after = jnp.where(at_right, after, pltpu.roll(after, 511, axis=1))
                    before = jnp.where(at_left, before, pltpu.roll(before, 1, axis=1))
                    balance = after - before + 4.0 * wu
                    if v == 4:
                        balance = balance + decay_ref[rows, :] * (q * q * inv)
                    across_ref[v, rows, :] = balance
                    ahead_ref[v, pl.ds(8 * t + 8, 8), :] = fy[v] - wu
                    behind_ref[v, pl.ds(8 * t + 8, 8), :] = fy[v] + wu
            last = segment == len(SEGMENT_WEIGHTS) - 1
            for t in (1, 2) if last else range(4):
                rows = pl.ds(8 * t, 8)
                step = weight * step_ref[n, rows, :]
                for v in range(5):
                    total = (
                        across_ref[v, rows, :]
                        + ahead_ref[v, pl.ds(8 * t + 9, 8), :]
                        - behind_ref[v, pl.ds(8 * t + 7, 8), :]
                        + source_ref[n, v, rows, :]
                    )
                    change = step * total
                    begin = start_ref[n, v, rows, :]
                    if last:
                        out_ref[n, v, pl.ds(8 * t - 8, 8), :] = -change
                        continue
                    after = begin - change
                    if t == 0:
                        after = jnp.where(is_first, begin, after)
                    if t == 3:
                        after = jnp.where(is_last, begin, after)
                    now_ref[n, v, rows, :] = after


def local(state, wall_distance, blade_counts):
    f32 = jnp.float32
    field = functools.partial(jax.ShapeDtypeStruct, dtype=f32)
    other = lax.ppermute(state, "zh", [(0, 1), (1, 0)])
    peak, counts, state = pl.pallas_call(
        peak_kernel, out_shape=(field((8, 1, 128)), field((2,)), field(state.shape)),
        in_specs=[SMEM, VMEM], out_specs=(VMEM, SMEM, VMEM),
        compiler_params=PARAMS, name="peak",
    )(blade_counts, state)
    peaks = lax.all_to_all(peak, "y", 0, 0)
    peak = pl.pallas_call(
        fold_kernel, out_shape=field((32, 1, 128)), in_specs=[VMEM], out_specs=VMEM,
        compiler_params=PARAMS, name="fold",
    )(peaks)
    peaks = lax.all_to_all(peak, ("zl", "zh", "core"), 0, 0)
    outer = pl.pallas_call(
        partial_kernel, out_shape=field((4, 136, 512)),
        in_specs=[SMEM, VMEM, VMEM, VMEM], out_specs=VMEM,
        scratch_shapes=[pltpu.VMEM((NT, 128), f32)],
        compiler_params=PARAMS, name="partial_sources",
    )(counts, state, other, peaks)
    outer = lax.all_to_all(outer, "x", 0, 0)
    far, near, inner = pl.pallas_call(
        edge_kernel, out_shape=(field((96, 512)), field((96, 512)), field((4, 80, 512))),
        in_specs=[SMEM] + [VMEM] * 4, out_specs=(VMEM, VMEM, VMEM),
        compiler_params=PARAMS, name="edges",
    )(counts, state, other, wall_distance, outer)
    count = lax.axis_size(CELLS)
    line = 2 * lax.axis_size("zl")
    across = []
    for i in range(1, count, 2):
        for half in range(2):
            there = 1 - half if (i + 1) % line == 0 else half
            across.append((2 * i + half, 2 * ((i + 1) % count) + there))
    far = lax.ppermute(far, CELLS + ("zh",), across + [(j, i) for i, j in across])
    near = lax.ppermute(near, "core", [(0, 1), (1, 0)])
    inner = lax.all_to_all(inner, "x", 0, 0)
    return pl.pallas_call(
        march_kernel, out_shape=field(state.shape),
        in_specs=[SMEM] + [VMEM] * 6, out_specs=VMEM,
        scratch_shapes=[
            pltpu.VMEM((2, 5, 32, 512), f32),
            pltpu.VMEM((2, 5, 32, 512), f32),
            pltpu.VMEM((2, 5, 32, 512), f32),
            pltpu.VMEM((2, 32, 512), f32),
            pltpu.VMEM((32, 512), f32),
            pltpu.VMEM((5, 32, 512), f32),
            pltpu.VMEM((5, 48, 512), f32),
            pltpu.VMEM((5, 48, 512), f32),
        ],
        compiler_params=PARAMS, name="march",
    )(counts, state, wall_distance, outer, inner, far, near)


def solution(mesh):
    fine = Mesh(mesh.devices.reshape(8, 8, 2, 4, 2), ("y", "zl", "core", "x", "zh"))
    inst = ("x", "zh")
    placed = (P(inst, None, CELLS, None), P(CELLS, None), P())
    return jax.shard_map(
        local, mesh=fine, in_specs=placed, out_specs=P(inst, None, CELLS, None), check_vma=False
    )
```

```python
import functools
import math

import jax
import jax.numpy as jnp
from jax import lax
from jax.experimental import pallas as pl
from jax.experimental.pallas import tpu as pltpu
from jax.sharding import Mesh
from jax.sharding import PartitionSpec as P

NT = 16
HALF = NT // 2
ROTATION = 0.001
SEGMENT_WEIGHTS = (0.25, 1.0 / 6.0, 0.375, 0.5, 1.0)
CELLS = ("y", "zl", "core")
VMEM = pl.BlockSpec(memory_space=pltpu.VMEM)
SMEM = pl.BlockSpec(memory_space=pltpu.SMEM)
PARAMS = pltpu.CompilerParams(vmem_limit_bytes=12 * 1024 * 1024)

SLOPE = [
    -(2.0 / NT) * sum(k * math.sin(2.0 * math.pi * k * j / NT) for k in range(1, HALF))
    for j in range(NT)
]


def omega_of(counts_ref):
    return (2.0 * math.pi * ROTATION) * counts_ref[1]


def speed_sum_and_max(r, mx, my, e):
    inv = 1.0 / r
    vx = mx * inv
    vy = my * inv
    p = 0.4 * (e - 0.5 * (mx * vx + my * vy))
    c = jnp.sqrt(1.4 * p * inv)
    ax = jnp.abs(vx)
    ay = jnp.abs(vy)
    return ax + ay + 2.0 * c, jnp.maximum(ax, ay) + c


def peak_kernel(whole_ref, state_ref, out_ref, counts_ref, held_ref):
    held_ref[...] = state_ref[...]
    for k in range(2):
        counts_ref[k] = whole_ref[k].astype(jnp.float32)
    best = None
    for n in range(2):
        for t in range(2):
            rows = pl.ds(8 * t, 8)
            _, top = speed_sum_and_max(*(state_ref[n, v, rows, :] for v in range(4)))
            best = top if best is None else jnp.maximum(best, top)
    peak = jnp.max(best, axis=(0, 1), keepdims=True)
    out_ref[...] = jnp.broadcast_to(peak[None], out_ref.shape)


def fold_kernel(peaks_ref, out_ref):
    peak = jnp.max(peaks_ref[...], axis=0)
    out_ref[...] = jnp.broadcast_to(peak[None], out_ref.shape)


def combine(counts_ref, fields, crossing, step, n):
    omega = omega_of(counts_ref)
    total = None
    for m, field in enumerate(fields):
        own, high, low = offsets(step, n, m)
        factor = SLOPE[own]
        if m >= 2:
            factor = jnp.where(crossing, SLOPE[high], SLOPE[low])
        term = (omega * factor) * field
        total = term if total is None else total + term
    return total


def add_partials(counts_ref, state_ref, other_ref, out_ref, edge):
    me_x = lax.axis_index("x")
    is_upper = lax.axis_index("zh") == 1
    is_even = lax.axis_index("core") == 0
    row = lax.broadcasted_iota(jnp.int32, (8, 512), 0)
    for v in range(5):
        fields = [
            jnp.where((row < 4) == edge, ref[m, v, 0:8, :], ref[m, v, 8:16, :])
            for ref in (state_ref, other_ref)
            for m in range(2)
        ]
        if edge:
            turned = [jnp.where(is_even, f, pltpu.roll(f, 4, axis=0)) for f in fields]
            turned = turned[2:] + turned[:2]
        for step in range(4):
            target = lax.rem(me_x + step, 4)
            for n in range(2):
                total = combine(counts_ref, fields, is_upper, step, n)
                out_ref[target, pl.ds((0 if edge else 136) + (n * 5 + v) * 8, 8), :] = total
            if edge:
                first, second = (
                    combine(counts_ref, turned, jnp.logical_not(is_upper), step, n)
                    for n in range(2)
                )
                out_ref[target, pl.ds(96 + v * 8, 8), :] = jnp.where(
                    row < 4, first, pltpu.roll(second, 4, axis=0)
                )


def offsets(step, n, m):
    apart = 4 * step + n - m % 2
    return apart % NT, (apart + 2) % NT, (apart - 2) % NT


def partial_kernel(counts_ref, state_ref, other_ref, peaks_ref, out_ref, lag_ref):
    me_x = lax.axis_index("x")
    is_lower = lax.axis_index("zh") == 0
    place = lax.axis_index(CELLS)
    is_last = place == lax.axis_size(CELLS) - 1
    add_partials(counts_ref, state_ref, other_ref, out_ref, True)
    add_partials(counts_ref, state_ref, other_ref, out_ref, False)
    ratio = jnp.full((NT, 128), counts_ref[1]) / jnp.full((NT, 128), counts_ref[0])
    sigma = 2.0 * math.pi * ratio
    shift = jnp.where(is_last, sigma, -sigma)
    offset = lax.broadcasted_iota(jnp.int32, (NT, 128), 0).astype(jnp.float32)
    order = lax.broadcasted_iota(jnp.int32, (NT, 128), 1)
    angle = (2.0 * math.pi / NT) * offset + shift
    share = jnp.where(order > HALF, 0.0, jnp.where((order == 0) | (order == HALF), 1.0, 2.0))
    terms = share * jnp.cos(order.astype(jnp.float32) * angle)
    lag_ref[...] = jnp.broadcast_to(
        jnp.sum(terms, axis=1, keepdims=True) * (1.0 / NT), lag_ref.shape
    )

    def lag(j):
        return jnp.concatenate([lag_ref[j : j + 1, :]] * 4, axis=1)

    peak = jnp.max(peaks_ref[...], axis=0)
    peak = jnp.broadcast_to(jnp.concatenate([peak] * 4, axis=1), (6, 512))
    for step in range(4):
        target = lax.rem(me_x + step, 4)
        for n in range(2):
            factor = []
            for m in range(4):
                own, high, low = offsets(step, n, m)
                factor.append(
                    lag(own) if m < 2 else jnp.where(is_lower, lag(high), lag(low))
                )
            for v in range(5):
                total = None
                for m, ref in enumerate((other_ref, other_ref, state_ref, state_ref)):
                    edge = jnp.where(is_last, ref[m % 2, v, 15:16, :], ref[m % 2, v, 0:1, :])
                    term = factor[m] * edge
                    total = term if total is None else total + term
                out_ref[target, pl.ds(80 + n * 5 + v, 1), :] = total
        out_ref[target, pl.ds(90, 6), :] = peak


def added(parts_ref, start, count):
    rows = pl.ds(start, count)
    return (parts_ref[0, rows, :] + parts_ref[1, rows, :]) + (
        parts_ref[2, rows, :] + parts_ref[3, rows, :]
    )


def edge_kernel(state_ref, other_ref, wall_ref, outer_ref, far_ref, near_ref):
    place = lax.axis_index(CELLS)
    is_first = place == 0
    is_last = place == lax.axis_size(CELLS) - 1
    is_even = lax.axis_index("core") == 0
    row = lax.broadcasted_iota(jnp.int32, (8, 512), 0)

    def put(rows, up, down):
        far_ref[rows, :] = jnp.where(is_even, down, up)
        near_ref[rows, :] = jnp.where(is_even, up, down)

    is_low_end = is_even & (lax.axis_index("zl") == 0)
    is_high_end = jnp.logical_not(is_even) & (
        lax.axis_index("zl") == lax.axis_size("zl") - 1
    )
    is_end = is_low_end | is_high_end
    near_half = (row < 4) == is_even
    for v in range(5):
        extra = added(outer_ref, 96 + v * 8, 8)
        turned = pltpu.roll(extra, 4, axis=0)
        for n in range(2):
            at = n * 5 + v
            rows = pl.ds(at * 8, 8)
            fifth = pl.ds(80 + at, 1)
            source = pltpu.roll(added(outer_ref, at * 8, 8), 4, axis=0)
            up = jnp.where(row >= 4, state_ref[n, v, 8:16, :], source)
            down = jnp.where(row < 4, state_ref[n, v, 0:8, :], source)
            near_ref[rows, :] = jnp.where(is_even, up, down)
            near_ref[fifth, :] = jnp.where(
                is_even, state_ref[n, v, 11:12, :], state_ref[n, v, 4:5, :]
            )
            far = jnp.where(is_even, down, up)
            lagged = jnp.broadcast_to(added(outer_ref, 80 + at, 1), (8, 512))
            theirs = jnp.where(is_even, other_ref[n, v, 0:8, :], other_ref[n, v, 8:16, :])
            source = jnp.where(is_even, turned, extra) if n == 0 else jnp.where(is_even, extra, turned)
            theirs = jnp.where(near_half, theirs, source)
            theirs = jnp.where((is_first & (row == 0)) | (is_last & (row == 7)), lagged, theirs)
            far_ref[rows, :] = jnp.where(is_end, theirs, far)
            low, high = (
                jnp.where(is_end, other_ref[n, v, k : k + 1, :], state_ref[n, v, k : k + 1, :])
                for k in (4, 11)
            )
            far_ref[fifth, :] = jnp.where(is_even, low, high)
    put(pl.ds(90, 4), wall_ref[12:16, :], wall_ref[0:4, :])
    put(pl.ds(94, 2), wall_ref[14:16, :], wall_ref[0:2, :])


def march_kernel(
    counts_ref,
    state_ref,
    wall_ref,
    outer_ref,
    far_ref,
    near_ref,
    out_ref,
    start_ref,
    now_ref,
    source_ref,
    step_ref,
    decay_ref,
    across_ref,
    ahead_ref,
    behind_ref,
):
    place = lax.axis_index(CELLS)
    is_first = place == 0
    is_last = place == lax.axis_size(CELLS) - 1
    omega = omega_of(counts_ref)
    row = lax.broadcasted_iota(jnp.int32, (8, 512), 0)
    column = lax.broadcasted_iota(jnp.int32, (8, 512), 1)
    at_left = column == 0
    at_right = column == 511
    is_even = lax.axis_index("core") == 0

    def lower(rows):
        return jnp.where(is_even, far_ref[rows, :], near_ref[rows, :])

    def upper(rows):
        return jnp.where(is_even, near_ref[rows, :], far_ref[rows, :])

    peak = outer_ref[0, 90:91, :]
    for k in range(1, 4):
        peak = jnp.maximum(peak, outer_ref[k, 90:91, :])
    wave = jnp.broadcast_to(peak, (8, 512))

    walls = [
        jnp.concatenate([lower(pl.ds(90, 4))] * 2, axis=0),
        wall_ref[0:8, :],
        wall_ref[8:16, :],
        jnp.concatenate([upper(pl.ds(90, 4))] * 2, axis=0),
    ]
    for t in range(4):
        decay_ref[pl.ds(8 * t, 8), :] = 0.8 / (walls[t] * walls[t])
    for n in range(2):
        for v in range(5):
            at = n * 5 + v
            packed = lower(pl.ds(at * 8, 8))
            fifth = jnp.broadcast_to(lower(pl.ds(80 + at, 1)), (8, 512))
            start_ref[n, v, 0:8, :] = jnp.where(row >= 4, packed, fifth)
            source_ref[n, v, 0:8, :] = 2.0 * pltpu.roll(packed, 4, axis=0)
            packed = upper(pl.ds(at * 8, 8))
            fifth = jnp.broadcast_to(upper(pl.ds(80 + at, 1)), (8, 512))
            start_ref[n, v, 24:32, :] = jnp.where(row < 4, packed, fifth)
            source_ref[n, v, 24:32, :] = 2.0 * pltpu.roll(packed, 4, axis=0)
            start_ref[n, v, 8:24, :] = state_ref[n, v, :, :]
            outer = 2.0 * added(outer_ref, at * 8, 8)
            inner = 2.0 * added(outer_ref, 136 + at * 8, 8)
            source_ref[n, v, 8:16, :] = jnp.where(row < 4, outer, inner)
            source_ref[n, v, 16:24, :] = jnp.where(row < 4, inner, outer)
        for t in range(4):
            rows = pl.ds(8 * t, 8)
            both, _ = speed_sum_and_max(*(start_ref[n, v, rows, :] for v in range(4)))
            step_ref[n, rows, :] = 0.5 / (both + omega * HALF)

    for segment, weight in enumerate(SEGMENT_WEIGHTS):
        from_ref = start_ref if segment == 0 else now_ref
        for n in range(2):
            for t in range(4):
                rows = pl.ds(8 * t, 8)
                r, mx, my, e, q = (from_ref[n, v, rows, :] for v in range(5))
                inv = 1.0 / r
                vx = mx * inv
                vy = my * inv
                p = 0.4 * (e - 0.5 * (mx * vx + my * vy))
                h = e + p
                fx = (mx, mx * vx + p, my * vx, h * vx, q * vx)
                fy = (my, mx * vy, my * vy + p, h * vy, q * vy)
                for v, u in enumerate((r, mx, my, e, q)):
                    wu = wave * u
                    after = fx[v] - wu
                    before = fx[v] + wu
                    after = jnp.where(at_right, after, pltpu.roll(after, 511, axis=1))
                    before = jnp.where(at_left, before, pltpu.roll(before, 1, axis=1))
                    balance = after - before + 4.0 * wu
                    if v == 4:
                        balance = balance + decay_ref[rows, :] * (q * q * inv)
                    across_ref[v, rows, :] = balance
                    ahead_ref[v, pl.ds(8 * t + 8, 8), :] = fy[v] - wu
                    behind_ref[v, pl.ds(8 * t + 8, 8), :] = fy[v] + wu
            last = segment == len(SEGMENT_WEIGHTS) - 1
            for t in (1, 2) if last else range(4):
                rows = pl.ds(8 * t, 8)
                step = weight * step_ref[n, rows, :]
                for v in range(5):
                    total = (
                        across_ref[v, rows, :]
                        + ahead_ref[v, pl.ds(8 * t + 9, 8), :]
                        - behind_ref[v, pl.ds(8 * t + 7, 8), :]
                        + source_ref[n, v, rows, :]
                    )
                    change = step * total
                    begin = start_ref[n, v, rows, :]
                    if last:
                        out_ref[n, v, pl.ds(8 * t - 8, 8), :] = -change
                        continue
                    after = begin - change
                    if t == 0:
                        after = jnp.where(is_first, begin, after)
                    if t == 3:
                        after = jnp.where(is_last, begin, after)
                    now_ref[n, v, rows, :] = after


def local(state, wall_distance, blade_counts):
    f32 = jnp.float32
    field = functools.partial(jax.ShapeDtypeStruct, dtype=f32)
    other = lax.ppermute(state, "zh", [(0, 1), (1, 0)])
    peak, counts, state = pl.pallas_call(
        peak_kernel, out_shape=(field((8, 1, 128)), field((2,)), field(state.shape)),
        in_specs=[SMEM, VMEM], out_specs=(VMEM, SMEM, VMEM),
        compiler_params=PARAMS, name="peak",
    )(blade_counts, state)
    peaks = lax.all_to_all(peak, "y", 0, 0)
    peak = pl.pallas_call(
        fold_kernel, out_shape=field((32, 1, 128)), in_specs=[VMEM], out_specs=VMEM,
        compiler_params=PARAMS, name="fold",
    )(peaks)
    peaks = lax.all_to_all(peak, ("zl", "zh", "core"), 0, 0)
    outer = pl.pallas_call(
        partial_kernel, out_shape=field((4, 216, 512)),
        in_specs=[SMEM, VMEM, VMEM, VMEM], out_specs=VMEM,
        scratch_shapes=[pltpu.VMEM((NT, 128), f32)],
        compiler_params=PARAMS, name="partial_sources",
    )(counts, state, other, peaks)
    outer = lax.all_to_all(outer, "x", 0, 0)
    far, near = pl.pallas_call(
        edge_kernel, out_shape=(field((96, 512)), field((96, 512))),
        in_specs=[VMEM] * 4, out_specs=(VMEM, VMEM),
        compiler_params=PARAMS, name="edges",
    )(state, other, wall_distance, outer)
    count = lax.axis_size(CELLS)
    line = 2 * lax.axis_size("zl")
    across = []
    for i in range(1, count, 2):
        for half in range(2):
            there = 1 - half if (i + 1) % line == 0 else half
            across.append((2 * i + half, 2 * ((i + 1) % count) + there))
    far = lax.ppermute(far, CELLS + ("zh",), across + [(j, i) for i, j in across])
    near = lax.ppermute(near, "core", [(0, 1), (1, 0)])
    return pl.pallas_call(
        march_kernel, out_shape=field(state.shape),
        in_specs=[SMEM] + [VMEM] * 5, out_specs=VMEM,
        scratch_shapes=[
            pltpu.VMEM((2, 5, 32, 512), f32),
            pltpu.VMEM((2, 5, 32, 512), f32),
            pltpu.VMEM((2, 5, 32, 512), f32),
            pltpu.VMEM((2, 32, 512), f32),
            pltpu.VMEM((32, 512), f32),
            pltpu.VMEM((5, 32, 512), f32),
            pltpu.VMEM((5, 48, 512), f32),
            pltpu.VMEM((5, 48, 512), f32),
        ],
        compiler_params=PARAMS, name="march",
    )(counts, state, wall_distance, outer, far, near)


def solution(mesh):
    fine = Mesh(mesh.devices.reshape(8, 8, 2, 4, 2), ("y", "zl", "core", "x", "zh"))
    inst = ("x", "zh")
    placed = (P(inst, None, CELLS, None), P(CELLS, None), P())
    return jax.shard_map(
        local, mesh=fine, in_specs=placed, out_specs=P(inst, None, CELLS, None), check_vma=False
    )
```

```python
import functools
import math

import jax
import jax.numpy as jnp
from jax import lax
from jax.experimental import pallas as pl
from jax.experimental.pallas import tpu as pltpu
from jax.sharding import Mesh
from jax.sharding import PartitionSpec as P

NT = 16
HALF = NT // 2
ROTATION = 0.001
SEGMENT_WEIGHTS = (0.25, 1.0 / 6.0, 0.375, 0.5, 1.0)
CELLS = ("y", "zl", "core")
VMEM = pl.BlockSpec(memory_space=pltpu.VMEM)
SMEM = pl.BlockSpec(memory_space=pltpu.SMEM)
PARAMS = pltpu.CompilerParams(vmem_limit_bytes=12 * 1024 * 1024)

SLOPE = [
    -(2.0 / NT) * sum(k * math.sin(2.0 * math.pi * k * j / NT) for k in range(1, HALF))
    for j in range(NT)
]


def omega_of(counts_ref):
    return (2.0 * math.pi * ROTATION) * counts_ref[1]


def speed_sum_and_max(r, mx, my, e):
    inv = 1.0 / r
    vx = mx * inv
    vy = my * inv
    p = 0.4 * (e - 0.5 * (mx * vx + my * vy))
    c = jnp.sqrt(1.4 * p * inv)
    ax = jnp.abs(vx)
    ay = jnp.abs(vy)
    return ax + ay + 2.0 * c, jnp.maximum(ax, ay) + c


def peak_kernel(whole_ref, state_ref, out_ref, counts_ref, held_ref):
    held_ref[...] = state_ref[...]
    for k in range(2):
        counts_ref[k] = whole_ref[k].astype(jnp.float32)
    best = None
    for n in range(2):
        for t in range(2):
            rows = pl.ds(8 * t, 8)
            _, top = speed_sum_and_max(*(state_ref[n, v, rows, :] for v in range(4)))
            best = top if best is None else jnp.maximum(best, top)
    peak = jnp.max(best, axis=(0, 1), keepdims=True)
    out_ref[...] = jnp.broadcast_to(peak[None], out_ref.shape)


def fold_kernel(peaks_ref, out_ref):
    peak = jnp.max(peaks_ref[...], axis=0)
    out_ref[...] = jnp.broadcast_to(peak[None], out_ref.shape)


def combine(counts_ref, fields, crossing, step, n):
    omega = omega_of(counts_ref)
    total = None
    for m, field in enumerate(fields):
        own, high, low = offsets(step, n, m)
        factor = SLOPE[own]
        if m >= 2:
            factor = jnp.where(crossing, SLOPE[high], SLOPE[low])
        term = (omega * factor) * field
        total = term if total is None else total + term
    return total


def add_partials(counts_ref, state_ref, other_ref, out_ref, edge):
    me_x = lax.axis_index("x")
    is_upper = lax.axis_index("zh") == 1
    is_even = lax.axis_index("core") == 0
    row = lax.broadcasted_iota(jnp.int32, (8, 512), 0)
    for v in range(5):
        fields = [
            jnp.where((row < 4) == edge, ref[m, v, 0:8, :], ref[m, v, 8:16, :])
            for ref in (state_ref, other_ref)
            for m in range(2)
        ]
        if edge:
            turned = [jnp.where(is_even, f, pltpu.roll(f, 4, axis=0)) for f in fields]
            turned = turned[2:] + turned[:2]
        for step in range(4):
            target = lax.rem(me_x + step, 4)
            for n in range(2):
                total = combine(counts_ref, fields, is_upper, step, n)
                out_ref[target, pl.ds((n * 5 + v) * 8, 8), :] = total
            if edge:
                first, second = (
                    combine(counts_ref, turned, jnp.logical_not(is_upper), step, n)
                    for n in range(2)
                )
                out_ref[target, pl.ds(80 + v * 8, 8), :] = jnp.where(
                    row < 4, first, pltpu.roll(second, 4, axis=0)
                )


def offsets(step, n, m):
    apart = 4 * step + n - m % 2
    return apart % NT, (apart + 2) % NT, (apart - 2) % NT


def partial_kernel(counts_ref, state_ref, other_ref, _, out_ref, lag_ref):
    me_x = lax.axis_index("x")
    is_lower = lax.axis_index("zh") == 0
    place = lax.axis_index(CELLS)
    is_last = place == lax.axis_size(CELLS) - 1
    add_partials(counts_ref, state_ref, other_ref, out_ref, True)
    ratio = jnp.full((NT, 128), counts_ref[1]) / jnp.full((NT, 128), counts_ref[0])
    sigma = 2.0 * math.pi * ratio
    shift = jnp.where(is_last, sigma, -sigma)
    offset = lax.broadcasted_iota(jnp.int32, (NT, 128), 0).astype(jnp.float32)
    order = lax.broadcasted_iota(jnp.int32, (NT, 128), 1)
    angle = (2.0 * math.pi / NT) * offset + shift
    share = jnp.where(order > HALF, 0.0, jnp.where((order == 0) | (order == HALF), 1.0, 2.0))
    terms = share * jnp.cos(order.astype(jnp.float32) * angle)
    lag_ref[...] = jnp.broadcast_to(
        jnp.sum(terms, axis=1, keepdims=True) * (1.0 / NT), lag_ref.shape
    )

    def lag(j):
        return jnp.concatenate([lag_ref[j : j + 1, :]] * 4, axis=1)

    row = lax.broadcasted_iota(jnp.int32, (8, 512), 0)

    @pl.when((place == 0) | is_last)
    def _():
        for step in range(4):
            target = lax.rem(me_x + step, 4)
            for v in range(5):
                totals = []
                for n in range(2):
                    total = None
                    for m, ref in enumerate((other_ref, other_ref, state_ref, state_ref)):
                        own, high, low = offsets(step, n, m)
                        factor = (
                            lag(own) if m < 2 else jnp.where(is_lower, lag(high), lag(low))
                        )
                        edge = jnp.where(is_last, ref[m % 2, v, 15:16, :], ref[m % 2, v, 0:1, :])
                        term = factor * edge
                        total = term if total is None else total + term
                    totals.append(jnp.broadcast_to(total, (8, 512)))
                out_ref[target, pl.ds(80 + v * 8, 8), :] = jnp.where(row < 4, *totals)


def added(parts_ref, start, count):
    rows = pl.ds(start, count)
    return (parts_ref[0, rows, :] + parts_ref[1, rows, :]) + (
        parts_ref[2, rows, :] + parts_ref[3, rows, :]
    )


def edge_kernel(counts_ref, state_ref, other_ref, wall_ref, outer_ref, far_ref, near_ref, inner_ref):
    place = lax.axis_index(CELLS)
    is_first = place == 0
    is_last = place == lax.axis_size(CELLS) - 1
    is_even = lax.axis_index("core") == 0
    row = lax.broadcasted_iota(jnp.int32, (8, 512), 0)

    def put(rows, up, down):
        far_ref[rows, :] = jnp.where(is_even, down, up)
        near_ref[rows, :] = jnp.where(is_even, up, down)

    is_low_end = is_even & (lax.axis_index("zl") == 0)
    is_high_end = jnp.logical_not(is_even) & (
        lax.axis_index("zl") == lax.axis_size("zl") - 1
    )
    is_end = is_low_end | is_high_end
    near_half = (row < 4) == is_even
    for v in range(5):
        extra = added(outer_ref, 80 + v * 8, 8)
        turned = pltpu.roll(extra, 4, axis=0)
        for n in range(2):
            at = n * 5 + v
            rows = pl.ds(at * 8, 8)
            fifth = pl.ds(80 + at, 1)
            source = pltpu.roll(added(outer_ref, at * 8, 8), 4, axis=0)
            up = jnp.where(row >= 4, state_ref[n, v, 8:16, :], source)
            down = jnp.where(row < 4, state_ref[n, v, 0:8, :], source)
            near_ref[rows, :] = jnp.where(is_even, up, down)
            near_ref[fifth, :] = jnp.where(
                is_even, state_ref[n, v, 11:12, :], state_ref[n, v, 4:5, :]
            )
            far = jnp.where(is_even, down, up)
            lagged = jnp.broadcast_to(extra[4 * n : 4 * n + 1, :], (8, 512))
            theirs = jnp.where(is_even, other_ref[n, v, 0:8, :], other_ref[n, v, 8:16, :])
            source = jnp.where(is_even, turned, extra) if n == 0 else jnp.where(is_even, extra, turned)
            theirs = jnp.where(near_half, theirs, source)
            theirs = jnp.where((is_first & (row == 0)) | (is_last & (row == 7)), lagged, theirs)
            far_ref[rows, :] = jnp.where(is_end, theirs, far)
            low, high = (
                jnp.where(is_end, other_ref[n, v, k : k + 1, :], state_ref[n, v, k : k + 1, :])
                for k in (4, 11)
            )
            far_ref[fifth, :] = jnp.where(is_even, low, high)
    put(pl.ds(90, 4), wall_ref[12:16, :], wall_ref[0:4, :])
    put(pl.ds(94, 2), wall_ref[14:16, :], wall_ref[0:2, :])
    add_partials(counts_ref, state_ref, other_ref, inner_ref, False)


def march_kernel(
    counts_ref,
    state_ref,
    wall_ref,
    outer_ref,
    inner_ref,
    far_ref,
    near_ref,
    peaks_ref,
    out_ref,
    start_ref,
    now_ref,
    source_ref,
    step_ref,
    decay_ref,
    across_ref,
    ahead_ref,
    behind_ref,
):
    place = lax.axis_index(CELLS)
    is_first = place == 0
    is_last = place == lax.axis_size(CELLS) - 1
    omega = omega_of(counts_ref)
    row = lax.broadcasted_iota(jnp.int32, (8, 512), 0)
    column = lax.broadcasted_iota(jnp.int32, (8, 512), 1)
    at_left = column == 0
    at_right = column == 511
    is_even = lax.axis_index("core") == 0

    def lower(rows):
        return jnp.where(is_even, far_ref[rows, :], near_ref[rows, :])

    def upper(rows):
        return jnp.where(is_even, near_ref[rows, :], far_ref[rows, :])

    peak = jnp.max(peaks_ref[...], axis=0)
    peak = jnp.concatenate([peak] * 4, axis=1)
    wave = jnp.broadcast_to(peak, (8, 512))

    walls = [
        jnp.concatenate([lower(pl.ds(90, 4))] * 2, axis=0),
        wall_ref[0:8, :],
        wall_ref[8:16, :],
        jnp.concatenate([upper(pl.ds(90, 4))] * 2, axis=0),
    ]
    for t in range(4):
        decay_ref[pl.ds(8 * t, 8), :] = 0.8 / (walls[t] * walls[t])
    for n in range(2):
        for v in range(5):
            at = n * 5 + v
            packed = lower(pl.ds(at * 8, 8))
            fifth = jnp.broadcast_to(lower(pl.ds(80 + at, 1)), (8, 512))
            start_ref[n, v, 0:8, :] = jnp.where(row >= 4, packed, fifth)
            source_ref[n, v, 0:8, :] = 2.0 * pltpu.roll(packed, 4, axis=0)
            packed = upper(pl.ds(at * 8, 8))
            fifth = jnp.broadcast_to(upper(pl.ds(80 + at, 1)), (8, 512))
            start_ref[n, v, 24:32, :] = jnp.where(row < 4, packed, fifth)
            source_ref[n, v, 24:32, :] = 2.0 * pltpu.roll(packed, 4, axis=0)
            start_ref[n, v, 8:24, :] = state_ref[n, v, :, :]
            outer = 2.0 * added(outer_ref, at * 8, 8)
            inner = 2.0 * added(inner_ref, at * 8, 8)
            source_ref[n, v, 8:16, :] = jnp.where(row < 4, outer, inner)
            source_ref[n, v, 16:24, :] = jnp.where(row < 4, inner, outer)
        for t in range(4):
            rows = pl.ds(8 * t, 8)
            both, _ = speed_sum_and_max(*(start_ref[n, v, rows, :] for v in range(4)))
            step_ref[n, rows, :] = 0.5 / (both + omega * HALF)

    for segment, weight in enumerate(SEGMENT_WEIGHTS):
        from_ref = start_ref if segment == 0 else now_ref
        for n in range(2):
            for t in range(4):
                rows = pl.ds(8 * t, 8)
                r, mx, my, e, q = (from_ref[n, v, rows, :] for v in range(5))
                inv = 1.0 / r
                vx = mx * inv
                vy = my * inv
                p = 0.4 * (e - 0.5 * (mx * vx + my * vy))
                h = e + p
                fx = (mx, mx * vx + p, my * vx, h * vx, q * vx)
                fy = (my, mx * vy, my * vy + p, h * vy, q * vy)
                for v, u in enumerate((r, mx, my, e, q)):
                    wu = wave * u
                    after = fx[v] - wu
                    before = fx[v] + wu
                    after = jnp.where(at_right, after, pltpu.roll(after, 511, axis=1))
                    before = jnp.where(at_left, before, pltpu.roll(before, 1, axis=1))
                    balance = after - before + 4.0 * wu
                    if v == 4:
                        balance = balance + decay_ref[rows, :] * (q * q * inv)
                    across_ref[v, rows, :] = balance
                    ahead_ref[v, pl.ds(8 * t + 8, 8), :] = fy[v] - wu
                    behind_ref[v, pl.ds(8 * t + 8, 8), :] = fy[v] + wu
            last = segment == len(SEGMENT_WEIGHTS) - 1
            for t in (1, 2) if last else range(4):
                rows = pl.ds(8 * t, 8)
                step = weight * step_ref[n, rows, :]
                for v in range(5):
                    total = (
                        across_ref[v, rows, :]
                        + ahead_ref[v, pl.ds(8 * t + 9, 8), :]
                        - behind_ref[v, pl.ds(8 * t + 7, 8), :]
                        + source_ref[n, v, rows, :]
                    )
                    change = step * total
                    begin = start_ref[n, v, rows, :]
                    if last:
                        out_ref[n, v, pl.ds(8 * t - 8, 8), :] = -change
                        continue
                    after = begin - change
                    if t == 0:
                        after = jnp.where(is_first, begin, after)
                    if t == 3:
                        after = jnp.where(is_last, begin, after)
                    now_ref[n, v, rows, :] = after


def local(state, wall_distance, blade_counts):
    f32 = jnp.float32
    field = functools.partial(jax.ShapeDtypeStruct, dtype=f32)
    other = lax.ppermute(state, "zh", [(0, 1), (1, 0)])
    peak, counts, state = pl.pallas_call(
        peak_kernel, out_shape=(field((32, 1, 128)), field((2,)), field(state.shape)),
        in_specs=[SMEM, VMEM], out_specs=(VMEM, SMEM, VMEM),
        compiler_params=PARAMS, name="peak",
    )(blade_counts, state)
    peaks = lax.all_to_all(peak, ("y", "x"), 0, 0)
    peak = pl.pallas_call(
        fold_kernel, out_shape=field((32, 1, 128)), in_specs=[VMEM], out_specs=VMEM,
        compiler_params=PARAMS, name="fold",
    )(peaks)
    peaks = lax.all_to_all(peak, ("zl", "zh", "core"), 0, 0)
    outer = pl.pallas_call(
        partial_kernel, out_shape=field((4, 120, 512)),
        in_specs=[SMEM, VMEM, VMEM, VMEM], out_specs=VMEM,
        scratch_shapes=[pltpu.VMEM((NT, 128), f32)],
        compiler_params=PARAMS, name="partial_sources",
    )(counts, state, other, peaks)
    outer = lax.all_to_all(outer, "x", 0, 0)
    far, near, inner = pl.pallas_call(
        edge_kernel, out_shape=(field((96, 512)), field((96, 512)), field((4, 80, 512))),
        in_specs=[SMEM] + [VMEM] * 4, out_specs=(VMEM, VMEM, VMEM),
        compiler_params=PARAMS, name="edges",
    )(counts, state, other, wall_distance, outer)
    count = lax.axis_size(CELLS)
    line = 2 * lax.axis_size("zl")
    across = []
    for i in range(1, count, 2):
        for half in range(2):
            there = 1 - half if (i + 1) % line == 0 else half
            across.append((2 * i + half, 2 * ((i + 1) % count) + there))
    far = lax.ppermute(far, CELLS + ("zh",), across + [(j, i) for i, j in across])
    near = lax.ppermute(near, "core", [(0, 1), (1, 0)])
    inner = lax.all_to_all(inner, "x", 0, 0)
    return pl.pallas_call(
        march_kernel, out_shape=field(state.shape),
        in_specs=[SMEM] + [VMEM] * 7, out_specs=VMEM,
        scratch_shapes=[
            pltpu.VMEM((2, 5, 32, 512), f32),
            pltpu.VMEM((2, 5, 32, 512), f32),
            pltpu.VMEM((2, 5, 32, 512), f32),
            pltpu.VMEM((2, 32, 512), f32),
            pltpu.VMEM((32, 512), f32),
            pltpu.VMEM((5, 32, 512), f32),
            pltpu.VMEM((5, 48, 512), f32),
            pltpu.VMEM((5, 48, 512), f32),
        ],
        compiler_params=PARAMS, name="march",
    )(counts, state, wall_distance, outer, inner, far, near, peaks)


def solution(mesh):
    fine = Mesh(mesh.devices.reshape(8, 8, 2, 4, 2), ("y", "zl", "core", "x", "zh"))
    inst = ("x", "zh")
    placed = (P(inst, None, CELLS, None), P(CELLS, None), P())
    return jax.shard_map(
        local, mesh=fine, in_specs=placed, out_specs=P(inst, None, CELLS, None), check_vma=False
    )
```
